32 devices in a mesh: recv: 8 (over z, y), send: 4 (over x, core).
Axes of the slice: x: 2, y: 2, z: 4, core: 2. Of those that a mesh axis runs over, the one named last changes fastest.
Arguments:
- nodes: bfloat16 [4096, 256], P('recv'), may hold values from -24 to 24
- frames: int32 [4096], replicated, may hold values from 0 to 59, never falling along the last dimension, each value on 1 to 256 neighbouring positions
- pairs: int32 [2, 128], P(None, ('recv', 'send')), may hold values from 0 to 31, as said below
- masks: int32 [128, 128], P(('recv', 'send')), may hold values from 0 to 1, as said below
- d_out: bfloat16 [4096, 256], P('recv'), may hold values from -6 to 6
- w_query: bfloat16 [256, 256], replicated, may hold values from -0.375 to 0.375
- w_key: bfloat16 [256, 256], replicated, may hold values from -0.375 to 0.375
- w_value: bfloat16 [256, 256], replicated, may hold values from -0.375 to 0.375
- w_left: bfloat16 [256, 128], replicated, may hold values from -0.375 to 0.375
- w_right: bfloat16 [256, 128], replicated, may hold values from -0.375 to 0.375
- frame_edge: bfloat16 [128], replicated, may hold values from -4 to 4
- w_bias: bfloat16 [8, 128], replicated, may hold values from -0.5 to 0.5
- w_edge_value: bfloat16 [128, 256], replicated, may hold values from -0.5 to 0.5
- w_out: bfloat16 [256, 256], replicated, may hold values from -0.375 to 0.375
Outputs:
- mixed: bfloat16 [4096, 256], P('recv')
- grad_nodes: float32 [4096, 256], P('recv')
- grad_bias: float32 [8, 128], replicated
- grad_edge_value: float32 [128, 256], replicated
The draws below stay inside these ranges and needn't reach their ends.
Inputs may be any that keep to these rules, and one draw needn't show every extreme that they name: `pairs`: row 0 holds a slot's receiver block, row 1 its sender block; block b belongs to recv index b // 4. The slots of the device at recv index r have receiver blocks r * 4 to r * 4 + 3. The sender blocks of one receiver block are distinct over all its slots and include the block itself, in a slot at send index 0. On each device, the slots whose sender block belongs to another recv index name blocks of distinct recv indices. `masks`: A slot that pairs a block with itself is all ones; other slots may be all zeros. `frames`: frame ids never fall along the residues; every frame holds a residue.
All inputs are finite; a program needn't handle non-finite values.
Results may differ from the reference program's by a relative error of at most 0.039.
Values may be sent and summed in bfloat16 or wider, within the bound.
A program may use at most 128 MiB of HBM per device.

```python
import math
import jax
import jax.numpy as jnp
import numpy as np
from jax import lax

D = 256
E = 128
HEADS = 8
HEAD_DIM = 32
BLK = 128
FRAMES = 60
NB_DEV = 4
PAIRS_DEV = 4
NBLK = 32
NODES = 4096
SLOTS = 128
ATT_WIDTH = 256


def slot_layout():
    n_recv = NBLK // NB_DEV
    n_send = SLOTS // (PAIRS_DEV * n_recv)
    slot_index = jnp.arange(SLOTS, dtype=jnp.int32)
    device = slot_index // PAIRS_DEV
    within = slot_index % PAIRS_DEV
    recv_index = device // n_send
    send_index = device % n_send
    recv_block = recv_index * NB_DEV + within % NB_DEV
    slot_rank = send_index * (PAIRS_DEV // NB_DEV) + within // NB_DEV
    return (recv_block, slot_rank, recv_index, send_index, within)


def draw_pairs(key, part):
    n_recv = NBLK // NB_DEV
    recv_block, slot_rank, recv_index, send_index, within = slot_layout()
    spread = send_index * PAIRS_DEV + within - NB_DEV
    is_self = spread < 0
    offset_base = jnp.maximum(spread, 0)
    offset_rank = offset_base % (n_recv - 1)
    cycle = offset_base // (n_recv - 1)
    coin_bits = jax.random.randint(jax.random.fold_in(key, 11), (n_recv, n_recv - 1), 0, 1 << 20)
    column = jnp.arange(n_recv - 1, dtype=jnp.int32)
    scores = coin_bits * (n_recv - 1) + column[None, :]
    order = jnp.argsort(scores, axis=1, stable=True).astype(jnp.int32)
    offset = order[recv_index, offset_rank] + 1
    turn = jax.random.randint(jax.random.fold_in(key, 12), (NBLK,), 0, NB_DEV)
    owner = (recv_index + offset) % n_recv
    member = (cycle + turn[recv_block]) % NB_DEV
    send_block = jnp.where(is_self, recv_block, owner * NB_DEV + member)
    return jnp.stack([recv_block, send_block]).astype(jnp.int32)


def draw_masks(key, part):
    recv_block, slot_rank, recv_index, send_index, within = slot_layout()
    empty = jax.random.randint(jax.random.fold_in(key, 21), (SLOTS,), 0, 5) < 2
    live = jax.random.randint(jax.random.fold_in(key, 22), (SLOTS, BLK), 0, 4) < 3
    live = jnp.where(empty[:, None], False, live)
    live = jnp.where((slot_rank == 0)[:, None], True, live)
    return live.astype(jnp.int32)


def draw_nodes(key, part):
    return jnp.clip(jax.random.normal(jax.random.fold_in(key, 33), (NODES, D), jnp.float32), -6.0, 6.0).astype(jnp.bfloat16)


def query_key_base(key):
    first = jnp.clip(jax.random.normal(jax.random.fold_in(key, 41), (D, ATT_WIDTH), jnp.float32), -6.0, 6.0)
    second = jnp.clip(jax.random.normal(jax.random.fold_in(key, 42), (D, ATT_WIDTH), jnp.float32), -6.0, 6.0)
    return (first, second)


def draw_w_query(key, part):
    first, second = query_key_base(key)
    return (first * D ** (-0.5)).astype(jnp.bfloat16)


def draw_w_key(key, part):
    first, second = query_key_base(key)
    joined = second
    return (joined * D ** (-0.5)).astype(jnp.bfloat16)


def level_of(own_key, dims, cuts, least, top_value):
    def one(position, blocks):
        draws = jax.random.uniform(jax.random.fold_in(jax.random.fold_in(own_key, 6), position), (blocks,), jnp.float32, least / len(cuts), top_value / len(cuts))
        return jnp.repeat(jnp.exp(draws), dims[position] // blocks).reshape((-1,) + (1,) * (len(dims) - position - 1))

    loudness = one(*cuts[0])
    for cut in cuts[1:]:
        loudness = loudness * one(*cut)
    return loudness


def split_up(amount, total, limit, slope):
    portions = [(1 << 20) // math.isqrt(grade ** slope) + 1 for grade in range(2, amount + 1)]
    spare, holding = total - limit - (amount - 1), [1] * (amount - 1)
    while spare > 0:
        free = [i for i in range(amount - 1) if holding[i] < limit]
        whole, left = sum([portions[i] for i in free]), spare
        for i in free:
            extra = min(limit - holding[i], max(1, left * portions[i] // whole), spare)
            holding[i] = holding[i] + extra
            spare = spare - extra
    return np.array([limit] + holding)


def uneven_parts(stream_key, amount, total, bound, lean):
    if amount == 2:
        one = jax.random.randint(stream_key, (), max(1, total - bound), min(bound, total - 1) + 1)
        return jnp.stack([one, total - one])
    lengths = jnp.asarray(split_up(amount, total, bound, lean), jnp.int32)
    couples = (amount - 1) // 2
    giver, taker = lengths[1:1 + 2 * couples:2], lengths[2:2 + 2 * couples:2]
    slack = jnp.minimum(giver - 1, bound - taker)
    shifted = jax.random.randint(jax.random.fold_in(stream_key, 1), (couples,), 0, 1 << 20) % (slack + 1)
    lengths = lengths.at[1:1 + 2 * couples:2].set(giver - shifted).at[2:2 + 2 * couples:2].set(taker + shifted)
    return lengths[jax.random.permutation(jax.random.fold_in(stream_key, 2), amount)]


def bell_draw(rng, dims, width, most, pieces=(), held_as=jnp.bfloat16):
    level = level_of(rng, dims, pieces, -0.22, 0.18) if pieces else 1.0
    result = jax.random.normal(rng, dims, jnp.float32) * width * level
    return jnp.minimum(jnp.maximum(result, -most), most).astype(held_as)


def setup_inputs(seed: int = 0) -> dict:
    streams_of = jax.random.split(jax.random.key(seed), 15)
    return {
        "nodes": draw_nodes(jax.random.fold_in(streams_of[14], 71), 0),
        "frames": jnp.searchsorted(jnp.cumsum(uneven_parts(streams_of[1], FRAMES, NODES, NODES // 16, 0)), jnp.arange(NODES), side="right").astype(jnp.int32),
        "pairs": draw_pairs(jax.random.fold_in(streams_of[14], 71), 0),
        "masks": draw_masks(jax.random.fold_in(streams_of[14], 71), 0),
        "d_out": bell_draw(streams_of[4], (NODES, D), 1.0, 6.0, ((0, 8),)),
        "w_query": draw_w_query(jax.random.fold_in(streams_of[14], 71), 0),
        "w_key": draw_w_key(jax.random.fold_in(streams_of[14], 71), 0),
        "w_value": bell_draw(streams_of[7], (D, ATT_WIDTH), D ** -0.5, 0.375),
        "w_left": bell_draw(streams_of[8], (D, E), D ** -0.5, 0.375),
        "w_right": bell_draw(streams_of[9], (D, E), D ** -0.5, 0.375),
        "frame_edge": bell_draw(streams_of[10], (E,), 1.0, 4.0),
        "w_bias": bell_draw(streams_of[11], (HEADS, E), E ** -0.5, 0.5),
        "w_edge_value": bell_draw(streams_of[12], (E, ATT_WIDTH), E ** -0.5, 0.5),
        "w_out": bell_draw(streams_of[13], (ATT_WIDTH, D), ATT_WIDTH ** -0.5, 0.375),
    }


NEG_LARGE = -1.0e30


def highest(grad_rows, weight):
    return jnp.dot(grad_rows, weight.astype(jnp.float32).T, precision=lax.Precision.HIGHEST)


def add_rows(array, start, update):
    current = lax.dynamic_slice_in_dim(array, start, update.shape[0], 0)
    return lax.dynamic_update_slice_in_dim(array, current + update, start, 0)


def reference(nodes, frames, pairs, masks, d_out, w_query, w_key, w_value, w_left, w_right, frame_edge, w_bias, w_edge_value, w_out):
    def project(weight):
        return jnp.dot(nodes, weight, preferred_element_type=jnp.float32).astype(jnp.bfloat16)

    query = project(w_query)
    keys_all = project(w_key)
    values_all = project(w_value)
    left_all = project(w_left)
    right_all = project(w_right)
    scale = HEAD_DIM ** -0.5
    edge_gain = frame_edge.astype(jnp.float32)
    bias_weight = w_bias.astype(jnp.float32)

    def rows_of(array, start):
        return lax.dynamic_slice_in_dim(array, start, BLK, 0)

    def fetch(slot_at):
        recv_block = pairs[0, slot_at].astype(jnp.int32)
        send_block = pairs[1, slot_at].astype(jnp.int32)
        recv_start = (recv_block * BLK).astype(jnp.int32)
        send_start = (send_block * BLK).astype(jnp.int32)
        query_blk = rows_of(query, recv_start).astype(jnp.float32).reshape(BLK, HEADS, HEAD_DIM)
        keys_blk = rows_of(keys_all, send_start).astype(jnp.float32).reshape(BLK, HEADS, HEAD_DIM)
        values_blk = rows_of(values_all, send_start).astype(jnp.float32).reshape(BLK, HEADS, HEAD_DIM)
        same_frame = (rows_of(frames, recv_start)[:, None] == rows_of(frames, send_start)[None, :]).astype(jnp.float32)
        pre_act = (rows_of(left_all, recv_start).astype(jnp.float32)[:, None, :]
                   + rows_of(right_all, send_start).astype(jnp.float32)[None, :, :]
                   + same_frame[:, :, None] * edge_gain[None, None, :])
        edge_feat = jax.nn.silu(pre_act).astype(jnp.bfloat16)
        valid = masks[slot_at] > 0
        logits = jnp.einsum("ihd,jhd->hij", query_blk, keys_blk) * scale
        logits = logits + jnp.einsum("ije,he->hij", edge_feat.astype(jnp.float32), bias_weight)
        logits = jnp.where(valid[None, None, :], logits, NEG_LARGE)
        return recv_block, recv_start, send_start, query_blk, keys_blk, values_blk, pre_act, edge_feat, valid, logits

    def stats_step(carry, slot_at):
        row_top, row_total = carry
        recv_block, recv_start, send_start, query_blk, keys_blk, values_blk, pre_act, edge_feat, valid, logits = fetch(slot_at)
        slot_top = jnp.max(logits, axis=2)
        slot_total = jnp.sum(jnp.where(valid[None, None, :], jnp.exp(logits - slot_top[:, :, None]), 0.0), axis=2)
        old_top = row_top[recv_block]
        old_total = row_total[recv_block]
        new_top = jnp.maximum(old_top, slot_top)
        new_total = old_total * jnp.exp(old_top - new_top) + slot_total * jnp.exp(slot_top - new_top)
        return (row_top.at[recv_block].set(new_top), row_total.at[recv_block].set(new_total)), None

    slot_ids = jnp.arange(SLOTS, dtype=jnp.int32)
    start_stats = (jnp.full((NBLK, HEADS, BLK), NEG_LARGE, jnp.float32), jnp.zeros((NBLK, HEADS, BLK), jnp.float32))
    (row_top, row_total), _ = lax.scan(stats_step, start_stats, slot_ids)

    def probs_of(logits, valid, recv_block):
        return jnp.where(valid[None, None, :], jnp.exp(logits - row_top[recv_block][:, :, None]) / row_total[recv_block][:, :, None], 0.0)

    def sum_step(carry, slot_at):
        out_acc, ctx_acc = carry
        recv_block, recv_start, send_start, query_blk, keys_blk, values_blk, pre_act, edge_feat, valid, logits = fetch(slot_at)
        weights = probs_of(logits, valid, recv_block).astype(jnp.bfloat16).astype(jnp.float32)
        part_out = jnp.einsum("hij,jhd->ihd", weights, values_blk).reshape(BLK, ATT_WIDTH)
        part_ctx = jnp.einsum("hij,ije->ihe", weights, edge_feat.astype(jnp.float32)).reshape(BLK, HEADS * E)
        return (add_rows(out_acc, recv_start, part_out), add_rows(ctx_acc, recv_start, part_ctx)), None

    start_sums = (jnp.zeros((NODES, ATT_WIDTH), jnp.float32), jnp.zeros((NODES, HEADS * E), jnp.float32))
    (out_sum, ctx_sum), _ = lax.scan(sum_step, start_sums, slot_ids)
    ctx_heads = ctx_sum.reshape(NODES, HEADS, E)
    edge_value = w_edge_value.astype(jnp.float32).reshape(E, HEADS, HEAD_DIM)
    carried = jnp.einsum("ihe,ehd->ihd", ctx_heads, edge_value, precision=lax.Precision.HIGHEST).reshape(NODES, ATT_WIDTH)
    attended = (out_sum + carried).astype(jnp.bfloat16)
    mixed = (nodes.astype(jnp.float32) + jnp.dot(attended, w_out, preferred_element_type=jnp.float32)).astype(jnp.bfloat16)

    d_att = jnp.dot(d_out, w_out.T, preferred_element_type=jnp.float32).astype(jnp.bfloat16)
    d_att_heads = d_att.astype(jnp.float32).reshape(NODES, HEADS, HEAD_DIM)
    d_ctx = jnp.einsum("ihd,ehd->ihe", d_att_heads, edge_value).astype(jnp.bfloat16)
    d_ctx_f = d_ctx.astype(jnp.float32)
    grad_edge_value = jnp.einsum("ihe,ihd->ehd", ctx_heads, d_att_heads, precision=lax.Precision.HIGHEST).reshape(E, ATT_WIDTH)
    delta = (jnp.sum(d_att_heads * out_sum.reshape(NODES, HEADS, HEAD_DIM), axis=2)
             + jnp.sum(d_ctx_f * ctx_heads, axis=2))

    def grad_step(carry, slot_at):
        grad_query, grad_left, grad_keys, grad_values, grad_right, grad_bias = carry
        recv_block, recv_start, send_start, query_blk, keys_blk, values_blk, pre_act, edge_feat, valid, logits = fetch(slot_at)
        probs = probs_of(logits, valid, recv_block)
        weights = probs.astype(jnp.bfloat16).astype(jnp.float32)
        datt_blk = rows_of(d_att_heads, recv_start)
        dctx_blk = rows_of(d_ctx_f, recv_start)
        delta_blk = rows_of(delta, recv_start)
        edge_f = edge_feat.astype(jnp.float32)
        d_prob = jnp.einsum("ihd,jhd->hij", datt_blk, values_blk) + jnp.einsum("ihe,ije->hij", dctx_blk, edge_f)
        d_logit = jnp.where(valid[None, None, :], probs * (d_prob - delta_blk.T[:, :, None]), 0.0)
        d_logit = d_logit.astype(jnp.bfloat16).astype(jnp.float32)
        part_query = (jnp.einsum("hij,jhd->ihd", d_logit, keys_blk) * scale).reshape(BLK, ATT_WIDTH)
        part_keys = (jnp.einsum("hij,ihd->jhd", d_logit, query_blk) * scale).reshape(BLK, ATT_WIDTH)
        part_values = jnp.einsum("hij,ihd->jhd", weights, datt_blk).reshape(BLK, ATT_WIDTH)
        grad_bias = grad_bias + jnp.einsum("hij,ije->he", d_logit, edge_f)
        d_edge = jnp.einsum("hij,he->ije", d_logit, bias_weight) + jnp.einsum("hij,ihe->ije", weights, dctx_blk)
        sigmoid_v = jax.nn.sigmoid(pre_act)
        d_pre = (d_edge * sigmoid_v * (1.0 + pre_act * (1.0 - sigmoid_v))).astype(jnp.bfloat16).astype(jnp.float32)
        grad_query = add_rows(grad_query, recv_start, part_query)
        grad_left = add_rows(grad_left, recv_start, jnp.sum(d_pre, axis=1))
        grad_keys = add_rows(grad_keys, send_start, part_keys)
        grad_values = add_rows(grad_values, send_start, part_values)
        grad_right = add_rows(grad_right, send_start, jnp.sum(d_pre, axis=0))
        return (grad_query, grad_left, grad_keys, grad_values, grad_right, grad_bias), None

    start_grads = (jnp.zeros((NODES, ATT_WIDTH), jnp.float32), jnp.zeros((NODES, E), jnp.float32),
                   jnp.zeros((NODES, ATT_WIDTH), jnp.float32), jnp.zeros((NODES, ATT_WIDTH), jnp.float32),
                   jnp.zeros((NODES, E), jnp.float32), jnp.zeros((HEADS, E), jnp.float32))
    (grad_query, grad_left, grad_keys, grad_values, grad_right, grad_bias), _ = lax.scan(grad_step, start_grads, slot_ids)
    grad_nodes = (d_out.astype(jnp.float32) + highest(grad_query, w_query) + highest(grad_keys, w_key)
                  + highest(grad_values, w_value) + highest(grad_left, w_left) + highest(grad_right, w_right))
    return mixed, grad_nodes, grad_bias, grad_edge_value
```

```python
import functools

import jax
import jax.numpy as jnp
from jax import lax
from jax.experimental import pallas as pl
from jax.experimental.pallas import tpu as pltpu
from jax.sharding import PartitionSpec as P

NEG_LARGE = -1e30
CHUNK = 16
F32 = jnp.float32
BF16 = jnp.bfloat16


def dot(first, second, first_dim=1, second_dim=0):
    return lax.dot_general(
        first, second, (((first_dim,), (second_dim,)), ((), ())), preferred_element_type=F32
    )


def to_column(row):
    count = row.shape[1]
    eye = lax.broadcasted_iota(jnp.int32, (count, count), 0) == lax.broadcasted_iota(
        jnp.int32, (count, count), 1
    )
    return jnp.sum(jnp.where(eye, row, 0.0), axis=1, keepdims=True)


def to_row(column):
    count = column.shape[0]
    eye = lax.broadcasted_iota(jnp.int32, (count, count), 0) == lax.broadcasted_iota(
        jnp.int32, (count, count), 1
    )
    return jnp.sum(jnp.where(eye, column, 0.0), axis=0, keepdims=True)


def head_mask(heads, width):
    return lax.broadcasted_iota(jnp.int32, (heads, width), 1) // (
        width // heads
    ) == lax.broadcasted_iota(jnp.int32, (heads, width), 0)


def spread(rows, heads):
    count, width = rows.shape
    mask = head_mask(heads, width)
    wide = jnp.where(mask[None], rows.astype(F32)[:, None, :], 0.0)
    return wide.reshape(count * heads, width).astype(BF16)


def gather_heads(wide, heads):
    count, width = wide.shape
    mask = head_mask(heads, width)
    return jnp.sum(jnp.where(mask[None], wide.reshape(count // heads, heads, width), 0.0), axis=1)


def forward_kernel(
    scale,
    local_ref,
    table_ref,
    recv_ref,
    send_ref,
    frames_ref,
    frame_row_ref,
    mask_ref,
    nodes_ref,
    dout_ref,
    sender_ref,
    wq_ref,
    wk_ref,
    wv_ref,
    wl_ref,
    wr_ref,
    fe_ref,
    wb_ref,
    wev_ref,
    wo_ref,
    logit_ref,
    dprob_ref,
    slope_ref,
    sums_ref,
    wide_ref,
    att_ref,
    stats_ref,
    left_s,
    edge_s,
    probs_s,
):
    slot = pl.program_id(0)
    heads, edge_width = wb_ref.shape
    block = nodes_ref.shape[0]
    nodes = nodes_ref[...]
    sender = sender_ref[0]
    query = dot(nodes, wq_ref[...]).astype(BF16)
    left_s[...] = dot(nodes, wl_ref[...]).astype(BF16).astype(F32) * 0.5
    datt = dot(dout_ref[...], wo_ref[...], 1, 1).astype(BF16)
    keys = dot(sender, wk_ref[...]).astype(BF16)
    values = dot(sender, wv_ref[...]).astype(BF16)
    right = dot(sender, wr_ref[...]).astype(BF16).astype(F32) * 0.5
    right_same = right + fe_ref[...].astype(F32) * 0.5
    frame_col = jnp.broadcast_to(
        to_column(frame_row_ref[0].astype(F32)), (block, edge_width)
    )
    datt_wide = spread(datt, heads)
    logit_ref[0] = (dot(spread(query, heads), keys, 1, 1) * scale).reshape(block, heads, block)
    dprob_ref[0] = dot(datt_wide, values, 1, 1).reshape(block, heads, block)
    dctx = dot(datt_wide, wev_ref[...], 1, 1).reshape(block, heads, edge_width)
    bias = jnp.broadcast_to(wb_ref[...].astype(F32)[None], dctx.shape)
    wide_ref[0] = jnp.concatenate([bias, dctx], axis=1).astype(BF16)
    recv_start = recv_ref[slot] * block

    def edge_step(group, carry):
        start = group * CHUNK
        left_rows = left_s[pl.ds(start, CHUNK), :]
        for step in range(CHUNK):
            at = start + step
            frame = frames_ref[recv_start + at].astype(F32)
            half = left_rows[step : step + 1] + jnp.where(frame_col == frame, right_same, right)
            turn = jnp.tanh(half)
            gain = half * turn
            edge = (half + gain).astype(BF16)
            slope_ref[0, at] = ((1.0 + turn) * (1.0 + half - gain)).astype(BF16)
            edge_s[at] = edge
            both = dot(wide_ref[0, at], edge, 1, 1)
            logit_ref[0, at] = logit_ref[0, at] + both[:heads]
            dprob_ref[0, at] = dprob_ref[0, at] + both[heads:]
        return carry

    lax.fori_loop(0, block // CHUNK, edge_step, 0)
    valid = mask_ref[0] > 0

    def soft_step(group, carry):
        start = group * CHUNK
        rows = pl.ds(start * heads, CHUNK * heads)
        logits = logit_ref[0, pl.ds(start, CHUNK)].reshape(CHUNK * heads, block)
        dprob = dprob_ref[0, pl.ds(start, CHUNK)].reshape(CHUNK * heads, block)
        logits = jnp.where(valid, logits, NEG_LARGE)
        top = jnp.max(logits, axis=1, keepdims=True)
        probs = jnp.where(valid, jnp.exp(logits - top), 0.0)
        weighted = probs * dprob
        stats_ref[0, 0, pl.ds(group, 1), :] = to_row(top)
        stats_ref[0, 1, pl.ds(group, 1), :] = to_row(jnp.sum(probs, axis=1, keepdims=True))
        stats_ref[0, 2, pl.ds(group, 1), :] = to_row(jnp.sum(weighted, axis=1, keepdims=True))
        probs_s[rows, :] = probs.astype(BF16)
        pair = jnp.concatenate(
            [probs.reshape(CHUNK, heads, block), weighted.reshape(CHUNK, heads, block)], axis=1
        ).astype(BF16)
        for step in range(CHUNK):
            at = start + step
            sums_ref[0, at] = dot(pair[step], edge_s[at]).astype(BF16)
        return carry

    lax.fori_loop(0, block // CHUNK, soft_step, 0)
    stats_ref[0, 3] = jnp.full(stats_ref.shape[2:], local_ref[slot].astype(F32), F32)
    ctx = sums_ref[0].astype(F32)[:, :heads].reshape(block * heads, edge_width).astype(BF16)
    att_ref[0] = gather_heads(dot(probs_s[...], values) + dot(ctx, wev_ref[...]), heads)


def backward_kernel(
    scale,
    local_ref,
    table_ref,
    mask_ref,
    nodes_ref,
    dout_ref,
    sender_ref,
    wq_ref,
    wk_ref,
    wv_ref,
    wl_ref,
    wr_ref,
    wo_ref,
    logit_ref,
    dprob_ref,
    slope_ref,
    sums_ref,
    wide_ref,
    att_in_ref,
    stats_ref,
    joined_ref,
    recv_grad_ref,
    send_grad_ref,
    att_ref,
    grad_ev_ref,
    grad_bias_ref,
    probs_s,
    dlogit_s,
    ctx_s,
    left_s,
    right_s,
):
    slot = pl.program_id(0)
    heads = logit_ref.shape[2]
    block = nodes_ref.shape[0]
    edge_width = wide_ref.shape[3]
    width = wq_ref.shape[1]
    mask = head_mask(heads, width)
    valid = mask_ref[0] > 0

    @pl.when(slot == 0)
    def _():
        grad_ev_ref[...] = jnp.zeros_like(grad_ev_ref)
        grad_bias_ref[...] = jnp.zeros_like(grad_bias_ref)

    right_s[...] = jnp.zeros_like(right_s)

    def step_group(group, carry):
        start = group * CHUNK
        rows = pl.ds(start * heads, CHUNK * heads)
        lse = joined_ref[0, 0, pl.ds(group, 1), :]
        lse_col = to_column(lse)
        delta_col = to_column(joined_ref[0, 1, pl.ds(group, 1), :])
        factor_col = to_column(jnp.exp(stats_ref[0, 0, pl.ds(group, 1), :] - lse))
        logits = logit_ref[0, pl.ds(start, CHUNK)].reshape(CHUNK * heads, block)
        dprob = dprob_ref[0, pl.ds(start, CHUNK)].reshape(CHUNK * heads, block)
        probs = jnp.where(valid, jnp.exp(logits - lse_col), 0.0)
        dlogit = probs * (dprob - delta_col)
        probs_s[rows, :] = probs.astype(BF16)
        dlogit_s[rows, :] = dlogit.astype(BF16)
        sums = sums_ref[0, pl.ds(start, CHUNK)].astype(F32)
        ctx = sums[:, :heads].reshape(CHUNK * heads, edge_width) * factor_col
        ctx_s[rows, :] = ctx.astype(BF16)
        moved = sums[:, heads:].reshape(CHUNK * heads, edge_width) * factor_col - ctx * delta_col
        grad_bias_ref[...] += jnp.sum(moved.reshape(CHUNK, heads, edge_width), axis=0)
        factor = jnp.sum(
            jnp.where(mask[None], factor_col.reshape(CHUNK, heads, 1), 0.0), axis=1
        )
        att_ref[0, pl.ds(start, CHUNK), :] = att_in_ref[0, pl.ds(start, CHUNK), :] * factor
        pair = jnp.concatenate(
            [dlogit.reshape(CHUNK, heads, block), probs.reshape(CHUNK, heads, block)], axis=1
        ).astype(BF16)
        right_sum = right_s[...]
        lefts = []
        for step in range(CHUNK):
            at = start + step
            d_edge = dot(pair[step], wide_ref[0, at], 0, 0)
            d_pre = d_edge * slope_ref[0, at].astype(F32)
            right_sum = right_sum + d_pre
            lefts.append(jnp.sum(d_pre, axis=0, keepdims=True))
        right_s[...] = right_sum
        left_s[pl.ds(start, CHUNK), :] = jnp.concatenate(lefts, axis=0)
        return carry

    lax.fori_loop(0, block // CHUNK, step_group, 0)
    nodes = nodes_ref[...]
    sender = sender_ref[0]
    query_wide = spread(dot(nodes, wq_ref[...]).astype(BF16), heads)
    datt_wide = spread(dot(dout_ref[...], wo_ref[...], 1, 1).astype(BF16), heads)
    keys = dot(sender, wk_ref[...]).astype(BF16)
    dlogit = dlogit_s[...]
    grad_query = gather_heads(dot(dlogit, keys), heads) * scale
    grad_keys = dot(dlogit, query_wide, 0, 0) * scale
    grad_values = dot(probs_s[...], datt_wide, 0, 0)
    recv_grad_ref[0] = dot(grad_query.astype(BF16), wq_ref[...], 1, 1) + 0.5 * dot(
        left_s[...].astype(BF16), wl_ref[...], 1, 1
    )
    send_grad_ref[0] = (
        dot(grad_keys.astype(BF16), wk_ref[...], 1, 1)
        + dot(grad_values.astype(BF16), wv_ref[...], 1, 1)
        + 0.5 * dot(right_s[...].astype(BF16), wr_ref[...], 1, 1)
    )
    grad_ev_ref[...] += dot(ctx_s[...], datt_wide, 0, 0)


def whole_spec(array):
    zeros = (0,) * array.ndim
    return pl.BlockSpec(array.shape, lambda slot, *_: zeros)


def slot_spec(shape):
    rest = (0,) * (len(shape) - 1)
    return pl.BlockSpec((1,) + tuple(shape[1:]), lambda slot, *_: (slot,) + rest)


def body(
    nodes,
    frames,
    pairs,
    masks,
    d_out,
    w_query,
    w_key,
    w_value,
    w_left,
    w_right,
    frame_edge,
    w_bias,
    w_edge_value,
    w_out,
):
    rows, width = nodes.shape
    slots, block = masks.shape
    nb_local = rows // block
    heads, edge_width = w_bias.shape
    att_width = w_query.shape[1]
    scale = (att_width // heads) ** (-0.5)
    my_recv = lax.axis_index("recv")
    n_recv = lax.axis_size("recv")
    base_block = my_recv * nb_local

    send_blocks = pairs[1]
    local_blocks = pairs[0] - base_block
    owners = send_blocks // nb_local
    remote = owners != my_recv
    owner_ids = jnp.arange(n_recv, dtype=jnp.int32)
    hits = (owners[None, :] == owner_ids[:, None]) & remote[None, :]
    wanted = jnp.sum(jnp.where(hits, (send_blocks % nb_local)[None, :], 0), axis=1)
    requested = lax.all_to_all(wanted, "recv", split_axis=0, concat_axis=0, tiled=True)
    node_blocks = nodes.reshape(nb_local, block, width)
    got = lax.all_to_all(
        jnp.take(node_blocks, requested, axis=0), "recv", split_axis=0, concat_axis=0, tiled=True
    )
    table = jnp.concatenate([node_blocks, got], axis=0)
    table_at = jnp.where(remote, nb_local + owners, send_blocks - base_block)

    frame_rows = frames.reshape(-1, 1, block)
    mask_rows = masks.reshape(slots, 1, block)
    edge_row = frame_edge.reshape(1, edge_width)
    recv_spec = pl.BlockSpec((block, width), lambda slot, local, *_: (local[slot], 0))
    sender_spec = pl.BlockSpec((1, block, width), lambda slot, local, at, *_: (at[slot], 0, 0))
    logit_shape = (slots, block, heads, block)
    sums_shape = (slots, block, 2 * heads, edge_width)
    slope_shape = (slots, block, block, edge_width)
    att_shape = (slots, block, att_width)
    stats_shape = (slots, 4, block * heads // 128, 128)
    weights = (w_query, w_key, w_value, w_left, w_right, edge_row, w_bias, w_edge_value, w_out)
    forward = pl.pallas_call(
        functools.partial(forward_kernel, scale),
        grid_spec=pltpu.PrefetchScalarGridSpec(
            num_scalar_prefetch=5,
            grid=(slots,),
            in_specs=[
                pl.BlockSpec((1, 1, block), lambda slot, local, at, recv, send, *_: (send[slot], 0, 0)),
                slot_spec(mask_rows.shape),
                recv_spec,
                recv_spec,
                sender_spec,
            ]
            + [whole_spec(weight) for weight in weights],
            out_specs=[
                slot_spec(shape)
                for shape in (
                    logit_shape, logit_shape, slope_shape, sums_shape, sums_shape, att_shape, stats_shape,
                )
            ],
            scratch_shapes=[
                pltpu.VMEM((block, edge_width), F32),
                pltpu.VMEM((block, block, edge_width), BF16),
                pltpu.VMEM((block * heads, block), BF16),
            ],
        ),
        out_shape=[
            jax.ShapeDtypeStruct(logit_shape, F32),
            jax.ShapeDtypeStruct(logit_shape, F32),
            jax.ShapeDtypeStruct(slope_shape, BF16),
            jax.ShapeDtypeStruct(sums_shape, BF16),
            jax.ShapeDtypeStruct(sums_shape, BF16),
            jax.ShapeDtypeStruct(att_shape, F32),
            jax.ShapeDtypeStruct(stats_shape, F32),
        ],
        compiler_params=pltpu.CompilerParams(vmem_limit_bytes=50 * 2**20),
        name="forward",
    )
    logits, dprobs, slopes, sums, wides, att_parts, stats = forward(
        local_blocks, table_at, pairs[0], send_blocks, frames,
        frame_rows, mask_rows, nodes, d_out, table, *weights,
    )

    all_stats = lax.all_gather(stats, "send").reshape((-1,) + stats.shape[1:])
    lands = all_stats[:, 3, 0, 0].astype(jnp.int32)
    here = (lands[None, :] == local_blocks[:, None])[:, :, None, None]
    tops = all_stats[None, :, 0]
    top = jnp.max(jnp.where(here, tops, NEG_LARGE), axis=1)
    shares = jnp.where(here, jnp.exp(tops - top[:, None]), 0.0)
    total = jnp.sum(shares * all_stats[None, :, 1], axis=1)
    delta = jnp.sum(shares * all_stats[None, :, 2], axis=1) / total
    joined = jnp.stack([top + jnp.log(total), delta], axis=1)

    weights = (w_query, w_key, w_value, w_left, w_right, w_out)
    grad_shape = (slots, block, width)
    backward = pl.pallas_call(
        functools.partial(backward_kernel, scale),
        grid_spec=pltpu.PrefetchScalarGridSpec(
            num_scalar_prefetch=2,
            grid=(slots,),
            in_specs=[slot_spec(mask_rows.shape), recv_spec, recv_spec, sender_spec]
            + [whole_spec(weight) for weight in weights]
            + [
                slot_spec(shape)
                for shape in (
                    logit_shape, logit_shape, slope_shape, sums_shape, sums_shape, att_shape, stats_shape,
                    joined.shape,
                )
            ],
            out_specs=[
                slot_spec(grad_shape),
                slot_spec(grad_shape),
                slot_spec(att_shape),
                whole_spec(w_edge_value),
                whole_spec(w_bias),
            ],
            scratch_shapes=[
                pltpu.VMEM((block * heads, block), BF16),
                pltpu.VMEM((block * heads, block), BF16),
                pltpu.VMEM((block * heads, edge_width), BF16),
                pltpu.VMEM((block, edge_width), F32),
                pltpu.VMEM((block, edge_width), F32),
            ],
        ),
        out_shape=[
            jax.ShapeDtypeStruct(grad_shape, F32),
            jax.ShapeDtypeStruct(grad_shape, F32),
            jax.ShapeDtypeStruct(att_shape, F32),
            jax.ShapeDtypeStruct(w_edge_value.shape, F32),
            jax.ShapeDtypeStruct(w_bias.shape, F32),
        ],
        compiler_params=pltpu.CompilerParams(vmem_limit_bytes=50 * 2**20),
        name="backward",
    )
    recv_grads, send_grads, att, grad_ev, grad_bias = backward(
        local_blocks, table_at, mask_rows, nodes, d_out, table, *weights,
        logits, dprobs, slopes, sums, wides, att_parts, stats, joined,
    )

    block_ids = jnp.arange(nb_local, dtype=jnp.int32)
    to_recv = (local_blocks[None, :] == block_ids[:, None])[:, :, None, None]
    own = (~remote & ((send_blocks - base_block)[None, :] == block_ids[:, None]))[:, :, None, None]
    away = hits[:, :, None, None]
    leaving = jnp.sum(jnp.where(away, send_grads[None], 0.0), axis=1).astype(BF16)
    back = lax.all_to_all(leaving, "recv", split_axis=0, concat_axis=0, tiled=True)
    landing = (requested[None, :] == block_ids[:, None])[:, :, None, None]
    node_part = (
        jnp.sum(jnp.where(to_recv, recv_grads[None], 0.0), axis=1)
        + jnp.sum(jnp.where(own, send_grads[None], 0.0), axis=1)
        + jnp.sum(jnp.where(landing, back[None].astype(F32), 0.0), axis=1)
    ).reshape(rows, width)
    att_part = jnp.sum(jnp.where(to_recv, att[None], 0.0), axis=1).reshape(rows, att_width)
    attended, node_grad = lax.psum((att_part, node_part), "send")
    mixed = (
        nodes.astype(F32) + jnp.dot(attended.astype(BF16), w_out, preferred_element_type=F32)
    ).astype(BF16)
    grad_nodes = d_out.astype(F32) + node_grad
    grad_bias, grad_ev = lax.psum((grad_bias, grad_ev), ("recv", "send"))
    return (mixed, grad_nodes, grad_bias, grad_ev)


def solution(mesh):
    in_specs = (
        P("recv", None),
        P(),
        P(None, ("recv", "send")),
        P(("recv", "send"), None),
        P("recv", None),
        P(),
        P(),
        P(),
        P(),
        P(),
        P(),
        P(),
        P(),
        P(),
    )
    out_specs = (P("recv", None), P("recv", None), P(), P())
    return jax.shard_map(body, mesh=mesh, in_specs=in_specs, out_specs=out_specs, check_vma=False)
```

```python
import functools

import jax
import jax.numpy as jnp
from jax import lax
from jax.experimental import pallas as pl
from jax.experimental.pallas import tpu as pltpu
from jax.sharding import PartitionSpec as P

NEG_LARGE = -1e30
CHUNK = 16
F32 = jnp.float32
BF16 = jnp.bfloat16


def dot(first, second, first_dim=1, second_dim=0):
    return lax.dot_general(
        first, second, (((first_dim,), (second_dim,)), ((), ())), preferred_element_type=F32
    )


def to_column(row):
    count = row.shape[1]
    eye = lax.broadcasted_iota(jnp.int32, (count, count), 0) == lax.broadcasted_iota(
        jnp.int32, (count, count), 1
    )
    return jnp.sum(jnp.where(eye, row, 0.0), axis=1, keepdims=True)


def to_row(column):
    count = column.shape[0]
    eye = lax.broadcasted_iota(jnp.int32, (count, count), 0) == lax.broadcasted_iota(
        jnp.int32, (count, count), 1
    )
    return jnp.sum(jnp.where(eye, column, 0.0), axis=0, keepdims=True)


def head_mask(heads, width):
    return lax.broadcasted_iota(jnp.int32, (heads, width), 1) // (
        width // heads
    ) == lax.broadcasted_iota(jnp.int32, (heads, width), 0)


def spread(rows, heads):
    count, width = rows.shape
    mask = head_mask(heads, width)
    wide = jnp.where(mask[None], rows.astype(F32)[:, None, :], 0.0)
    return wide.reshape(count * heads, width).astype(BF16)


def gather_heads(wide, heads):
    count, width = wide.shape
    mask = head_mask(heads, width)
    return jnp.sum(jnp.where(mask[None], wide.reshape(count // heads, heads, width), 0.0), axis=1)


def forward_kernel(
    scale,
    local_ref,
    table_ref,
    recv_ref,
    send_ref,
    frames_ref,
    frame_row_ref,
    mask_ref,
    nodes_ref,
    dout_ref,
    sender_ref,
    wq_ref,
    wk_ref,
    wv_ref,
    wl_ref,
    wr_ref,
    fe_ref,
    wb_ref,
    wev_ref,
    wo_ref,
    logit_ref,
    dprob_ref,
    slope_ref,
    sums_ref,
    wide_ref,
    att_ref,
    stats_ref,
    left_s,
    edge_s,
    probs_s,
):
    slot = pl.program_id(0)
    heads, edge_width = wb_ref.shape
    block = nodes_ref.shape[0]
    nodes = nodes_ref[...]
    sender = sender_ref[0]
    query = dot(nodes, wq_ref[...]).astype(BF16)
    left_s[...] = dot(nodes, wl_ref[...]).astype(BF16).astype(F32) * 0.5
    datt = dot(dout_ref[...], wo_ref[...], 1, 1).astype(BF16)
    keys = dot(sender, wk_ref[...]).astype(BF16)
    values = dot(sender, wv_ref[...]).astype(BF16)
    right = dot(sender, wr_ref[...]).astype(BF16).astype(F32) * 0.5
    right_same = right + fe_ref[...].astype(F32) * 0.5
    frame_col = jnp.broadcast_to(
        to_column(frame_row_ref[0].astype(F32)), (block, edge_width)
    )
    datt_wide = spread(datt, heads)
    logit_ref[0] = (dot(spread(query, heads), keys, 1, 1) * scale).reshape(block, heads, block)
    dprob_ref[0] = dot(datt_wide, values, 1, 1).reshape(block, heads, block)
    dctx = dot(datt_wide, wev_ref[...], 1, 1).reshape(block, heads, edge_width)
    bias = jnp.broadcast_to(wb_ref[...].astype(F32)[None], dctx.shape)
    wide_ref[0] = jnp.concatenate([bias, dctx], axis=1).astype(BF16)
    recv_start = recv_ref[slot] * block

    def edge_step(group, carry):
        start = group * CHUNK
        left_rows = left_s[pl.ds(start, CHUNK), :]
        for step in range(CHUNK):
            at = start + step
            frame = frames_ref[recv_start + at].astype(F32)
            half = left_rows[step : step + 1] + jnp.where(frame_col == frame, right_same, right)
            turn = jnp.tanh(half)
            gain = half * turn
            edge = (half + gain).astype(BF16)
            slope_ref[0, at] = ((1.0 + turn) * (1.0 + half - gain)).astype(BF16)
            edge_s[at] = edge
            both = dot(wide_ref[0, at], edge, 1, 1)
            logit_ref[0, at] = logit_ref[0, at] + both[:heads]
            dprob_ref[0, at] = dprob_ref[0, at] + both[heads:]
        return carry

    lax.fori_loop(0, block // CHUNK, edge_step, 0)
    valid = mask_ref[0] > 0

    def soft_step(group, carry):
        start = group * CHUNK
        rows = pl.ds(start * heads, CHUNK * heads)
        logits = logit_ref[0, pl.ds(start, CHUNK)].reshape(CHUNK * heads, block)
        dprob = dprob_ref[0, pl.ds(start, CHUNK)].reshape(CHUNK * heads, block)
        logits = jnp.where(valid, logits, NEG_LARGE)
        top = jnp.max(logits, axis=1, keepdims=True)
        probs = jnp.where(valid, jnp.exp(logits - top), 0.0)
        weighted = probs * dprob
        stats_ref[0, 0, pl.ds(group, 1), :] = to_row(top)
        stats_ref[0, 1, pl.ds(group, 1), :] = to_row(jnp.sum(probs, axis=1, keepdims=True))
        stats_ref[0, 2, pl.ds(group, 1), :] = to_row(jnp.sum(weighted, axis=1, keepdims=True))
        probs_s[rows, :] = probs.astype(BF16)
        pair = jnp.concatenate(
            [probs.reshape(CHUNK, heads, block), weighted.reshape(CHUNK, heads, block)], axis=1
        ).astype(BF16)
        for step in range(CHUNK):
            at = start + step
            sums_ref[0, at] = dot(pair[step], edge_s[at]).astype(BF16)
        return carry

    lax.fori_loop(0, block // CHUNK, soft_step, 0)
    stats_ref[0, 3] = jnp.full(stats_ref.shape[2:], local_ref[slot].astype(F32), F32)
    ctx = sums_ref[0].astype(F32)[:, :heads].reshape(block * heads, edge_width).astype(BF16)
    att_ref[0] = gather_heads(dot(probs_s[...], values) + dot(ctx, wev_ref[...]), heads)


def backward_kernel(
    scale,
    local_ref,
    table_ref,
    mask_ref,
    nodes_ref,
    dout_ref,
    sender_ref,
    wq_ref,
    wk_ref,
    wv_ref,
    wl_ref,
    wr_ref,
    wo_ref,
    logit_ref,
    dprob_ref,
    slope_ref,
    sums_ref,
    wide_ref,
    att_in_ref,
    stats_ref,
    joined_ref,
    node_ref,
    leaving_ref,
    att_ref,
    grad_ev_ref,
    grad_bias_ref,
    probs_s,
    dlogit_s,
    ctx_s,
    left_s,
    right_s,
):
    slot = pl.program_id(0)
    heads = logit_ref.shape[2]
    block = nodes_ref.shape[0]
    edge_width = wide_ref.shape[3]
    width = wq_ref.shape[1]
    mask = head_mask(heads, width)
    valid = mask_ref[0] > 0

    @pl.when(slot == 0)
    def _():
        grad_ev_ref[...] = jnp.zeros_like(grad_ev_ref)
        grad_bias_ref[...] = jnp.zeros_like(grad_bias_ref)
        node_ref[...] = jnp.zeros_like(node_ref)
        leaving_ref[...] = jnp.zeros_like(leaving_ref)
        att_ref[...] = jnp.zeros_like(att_ref)

    local = local_ref[slot]
    place = table_ref[slot]
    own_blocks = node_ref.shape[0]
    right_s[...] = jnp.zeros_like(right_s)

    def step_group(group, carry):
        start = group * CHUNK
        rows = pl.ds(start * heads, CHUNK * heads)
        lse = joined_ref[0, 0, pl.ds(group, 1), :]
        lse_col = to_column(lse)
        delta_col = to_column(joined_ref[0, 1, pl.ds(group, 1), :])
        factor_col = to_column(jnp.exp(stats_ref[0, 0, pl.ds(group, 1), :] - lse))
        logits = logit_ref[0, pl.ds(start, CHUNK)].reshape(CHUNK * heads, block)
        dprob = dprob_ref[0, pl.ds(start, CHUNK)].reshape(CHUNK * heads, block)
        probs = jnp.where(valid, jnp.exp(logits - lse_col), 0.0)
        dlogit = probs * (dprob - delta_col)
        probs_s[rows, :] = probs.astype(BF16)
        dlogit_s[rows, :] = dlogit.astype(BF16)
        sums = sums_ref[0, pl.ds(start, CHUNK)].astype(F32)
        ctx = sums[:, :heads].reshape(CHUNK * heads, edge_width) * factor_col
        ctx_s[rows, :] = ctx.astype(BF16)
        moved = sums[:, heads:].reshape(CHUNK * heads, edge_width) * factor_col - ctx * delta_col
        grad_bias_ref[...] += jnp.sum(moved.reshape(CHUNK, heads, edge_width), axis=0)
        factor = jnp.sum(
            jnp.where(mask[None], factor_col.reshape(CHUNK, heads, 1), 0.0), axis=1
        )
        att_ref[local, pl.ds(start, CHUNK), :] += att_in_ref[0, pl.ds(start, CHUNK), :] * factor
        pair = jnp.concatenate(
            [dlogit.reshape(CHUNK, heads, block), probs.reshape(CHUNK, heads, block)], axis=1
        ).astype(BF16)
        right_sum = right_s[...]
        lefts = []
        for step in range(CHUNK):
            at = start + step
            d_edge = dot(pair[step], wide_ref[0, at], 0, 0)
            d_pre = d_edge * slope_ref[0, at].astype(F32)
            right_sum = right_sum + d_pre
            lefts.append(jnp.sum(d_pre, axis=0, keepdims=True))
        right_s[...] = right_sum
        left_s[pl.ds(start, CHUNK), :] = jnp.concatenate(lefts, axis=0)
        return carry

    lax.fori_loop(0, block // CHUNK, step_group, 0)
    nodes = nodes_ref[...]
    sender = sender_ref[0]
    query_wide = spread(dot(nodes, wq_ref[...]).astype(BF16), heads)
    datt_wide = spread(dot(dout_ref[...], wo_ref[...], 1, 1).astype(BF16), heads)
    keys = dot(sender, wk_ref[...]).astype(BF16)
    dlogit = dlogit_s[...]
    grad_query = gather_heads(dot(dlogit, keys), heads) * scale
    grad_keys = dot(dlogit, query_wide, 0, 0) * scale
    grad_values = dot(probs_s[...], datt_wide, 0, 0)
    node_ref[local] += dot(grad_query.astype(BF16), wq_ref[...], 1, 1) + 0.5 * dot(
        left_s[...].astype(BF16), wl_ref[...], 1, 1
    )
    send_grad = (
        dot(grad_keys.astype(BF16), wk_ref[...], 1, 1)
        + dot(grad_values.astype(BF16), wv_ref[...], 1, 1)
        + 0.5 * dot(right_s[...].astype(BF16), wr_ref[...], 1, 1)
    )

    @pl.when(place < own_blocks)
    def _():
        node_ref[place] += send_grad

    @pl.when(place >= own_blocks)
    def _():
        leaving_ref[place - own_blocks] = send_grad.astype(BF16)

    grad_ev_ref[...] += dot(ctx_s[...], datt_wide, 0, 0)


MESH = pl.DeviceIdType.MESH


def peers_of(axis, count):
    me = lax.axis_index(axis)
    return me, [
        (offset, lax.rem(me + offset, count), lax.rem(me + count - offset, count))
        for offset in range(1, count)
    ]


def meet(groups):
    barrier = pltpu.get_barrier_semaphore()
    total = 0
    for axis, peers in groups:
        for _, target, _ in peers:
            pl.semaphore_signal(barrier, inc=1, device_id={axis: target}, device_id_type=MESH)
            total += 1
    pl.semaphore_wait(barrier, total)


def post(axis, peers, sems, source, landing):
    copies = []
    for offset, target, _ in peers:
        copy = pltpu.make_async_remote_copy(
            src_ref=source(target),
            dst_ref=landing,
            send_sem=sems.at[0, offset],
            recv_sem=sems.at[1, offset],
            device_id={axis: target},
            device_id_type=MESH,
        )
        copy.start()
        copies.append(copy)
    return copies


def fetch_kernel(n_recv, wanted_ref, nodes_ref, got_ref, asked_ref, ask_s, reply_s, got_s, ask_sems, reply_sems):
    me, peers = peers_of("recv", n_recv)
    meet([("recv", peers)])
    asks = post("recv", peers, ask_sems, lambda target: wanted_ref.at[target], ask_s.at[me])
    nodes = nodes_ref[...].astype(F32)
    for copy in asks:
        copy.wait_recv()
    replies = []
    for peer in peers:
        offset, target, _ = peer
        ask = ask_s[target][0:1, :]
        reply = nodes[0]
        for at in range(1, nodes.shape[0]):
            reply = jnp.where(ask == float(at), nodes[at], reply)
        reply_s[offset] = reply.astype(BF16)
        replies += post("recv", [peer], reply_sems, lambda target: reply_s.at[offset], got_s.at[me])
    asked_ref[...] = jnp.zeros_like(asked_ref)
    got_ref[...] = jnp.zeros_like(got_ref)
    for _, target, _ in peers:
        asked_ref[target] = ask_s[target]
    for copy, (_, _, source) in zip(replies, peers):
        copy.wait_recv()
        got_ref[source] = got_s[source]
    for copy in asks + replies:
        copy.wait_send()


def join_kernel(n_send, stats_ref, joined_ref, all_s, sems):
    me, peers = peers_of("send", n_send)
    meet([("send", peers)])
    copies = post("send", peers, sems, lambda target: stats_ref, all_s.at[me])
    slots = stats_ref.shape[0]
    all_s[me] = stats_ref[...]
    for copy in copies:
        copy.wait_recv()
    for slot in range(slots):
        lands = stats_ref[slot, 3]
        top = stats_ref[slot, 0]
        for device in range(n_send):
            for other in range(slots):
                top = jnp.maximum(
                    top,
                    jnp.where(all_s[device, other, 3] == lands, all_s[device, other, 0], NEG_LARGE),
                )
        total = jnp.zeros_like(top)
        delta = jnp.zeros_like(top)
        for device in range(n_send):
            for other in range(slots):
                part = jnp.where(
                    all_s[device, other, 3] == lands, jnp.exp(all_s[device, other, 0] - top), 0.0
                )
                total = total + part * all_s[device, other, 1]
                delta = delta + part * all_s[device, other, 2]
        joined_ref[slot, 0] = top + jnp.log(total)
        joined_ref[slot, 1] = delta / total
    for copy in copies:
        copy.wait_send()


def tail_kernel(
    n_recv,
    n_send,
    att_ref,
    node_ref,
    leaving_ref,
    asked_ref,
    ev_ref,
    bias_ref,
    nodes_ref,
    dout_ref,
    wo_ref,
    mixed_ref,
    grad_ref,
    bias_out_ref,
    ev_out_ref,
    back_s,
    out_a,
    in_a,
    mix_s,
    small_s,
    small_all,
    acc_s,
    out_n,
    in_n,
    fin_s,
    back_sems,
    a_sems,
    mix_sems,
    small_sems,
    small_all_sems,
    n_sems,
    fin_sems,
):
    row, row_peers = peers_of("recv", n_recv)
    col, col_peers = peers_of("send", n_send)
    blocks, block, width = node_ref.shape
    rows = blocks * block
    share = rows // n_send
    ev_share = ev_ref.shape[0] // n_send
    bias_rows = bias_ref.shape[0]
    meet([("recv", row_peers), ("send", col_peers)])
    backs = post("recv", row_peers, back_sems, lambda target: leaving_ref.at[target], back_s.at[row])
    for part in range(n_send):
        out_a[part, :share] = att_ref[part * share : (part + 1) * share].astype(BF16)
        out_a[part, share : share + ev_share] = ev_ref[
            part * ev_share : (part + 1) * ev_share
        ].astype(BF16)
        bias = bias_ref[...] if part == 0 else jnp.zeros_like(bias_ref)
        out_a[part, share + ev_share :] = bias.astype(BF16)
    sent_a = post("send", col_peers, a_sems, lambda target: out_a.at[target], in_a.at[col])
    acc_s[...] = node_ref[...].reshape(rows, width)
    total = out_a[col].astype(F32)
    for copy, (_, _, source) in zip(sent_a, col_peers):
        copy.wait_recv()
        total = total + in_a[source].astype(F32)
    small_s[row] = total[share:].astype(BF16)
    smalls = post("recv", row_peers, small_sems, lambda target: small_s.at[row], small_s.at[row])
    here = pl.ds(pl.multiple_of(col * share, share), share)
    mixed = nodes_ref[here, :].astype(F32) + dot(total[:share].astype(BF16), wo_ref[...])
    mix_s[col] = mixed.astype(BF16)
    mixes = post("send", col_peers, mix_sems, lambda target: mix_s.at[col], mix_s.at[col])
    for copy, (_, _, source) in zip(backs, row_peers):
        copy.wait_recv()
        asked = asked_ref[source][0:1, :]
        landed = back_s[source].astype(F32)
        for at in range(blocks):
            acc_s[at * block : (at + 1) * block, :] += jnp.where(asked == float(at), landed, 0.0)
    for part in range(n_send):
        out_n[part] = acc_s[part * share : (part + 1) * share, :].astype(BF16)
    sent_n = post("send", col_peers, n_sems, lambda target: out_n.at[target], in_n.at[col])
    for copy in smalls:
        copy.wait_recv()
    small = small_s[0].astype(F32)
    for at in range(1, n_recv):
        small = small + small_s[at].astype(F32)
    small_all[col] = small.astype(BF16)
    small_alls = post(
        "send", col_peers, small_all_sems, lambda target: small_all.at[col], small_all.at[col]
    )
    total = out_n[col].astype(F32)
    for copy, (_, _, source) in zip(sent_n, col_peers):
        copy.wait_recv()
        total = total + in_n[source].astype(F32)
    fin_s[col] = total.astype(BF16)
    fins = post("send", col_peers, fin_sems, lambda target: fin_s.at[col], fin_s.at[col])
    for copy in mixes:
        copy.wait_recv()
    mixed_ref[...] = mix_s[...].reshape(rows, width)
    for copy in small_alls:
        copy.wait_recv()
    for part in range(n_send):
        ev_out_ref[part * ev_share : (part + 1) * ev_share, :] = small_all[part, :ev_share].astype(F32)
    bias_out_ref[...] = small_all[0, ev_share : ev_share + bias_rows].astype(F32)
    for copy in fins:
        copy.wait_recv()
    for part in range(n_send):
        span = slice(part * share, (part + 1) * share)
        grad_ref[span, :] = dout_ref[span, :].astype(F32) + fin_s[part].astype(F32)
    for copy in backs + sent_a + smalls + mixes + sent_n + small_alls + fins:
        copy.wait_send()


def whole_spec(array):
    zeros = (0,) * array.ndim
    return pl.BlockSpec(array.shape, lambda slot, *_: zeros)


def slot_spec(shape):
    rest = (0,) * (len(shape) - 1)
    return pl.BlockSpec((1,) + tuple(shape[1:]), lambda slot, *_: (slot,) + rest)


def body(
    nodes,
    frames,
    pairs,
    masks,
    d_out,
    w_query,
    w_key,
    w_value,
    w_left,
    w_right,
    frame_edge,
    w_bias,
    w_edge_value,
    w_out,
):
    rows, width = nodes.shape
    slots, block = masks.shape
    nb_local = rows // block
    heads, edge_width = w_bias.shape
    att_width = w_query.shape[1]
    scale = (att_width // heads) ** (-0.5)
    my_recv = lax.axis_index("recv")
    n_recv = lax.axis_size("recv")
    n_send = lax.axis_size("send")
    base_block = my_recv * nb_local

    send_blocks = pairs[1]
    local_blocks = pairs[0] - base_block
    owners = send_blocks // nb_local
    remote = owners != my_recv
    owner_ids = jnp.arange(n_recv, dtype=jnp.int32)
    hits = (owners[None, :] == owner_ids[:, None]) & remote[None, :]
    wanted = jnp.sum(jnp.where(hits, (send_blocks % nb_local)[None, :], 0), axis=1)
    node_blocks = nodes.reshape(nb_local, block, width)
    in_vmem = pl.BlockSpec(memory_space=pltpu.VMEM)
    asks_shape = (n_recv, 8, width)
    wants = jnp.broadcast_to(wanted.astype(F32)[:, None, None], asks_shape)
    got, asked = pl.pallas_call(
        functools.partial(fetch_kernel, n_recv),
        in_specs=[in_vmem] * 2,
        out_specs=[in_vmem] * 2,
        out_shape=[
            jax.ShapeDtypeStruct((n_recv, block, width), BF16),
            jax.ShapeDtypeStruct(asks_shape, F32),
        ],
        scratch_shapes=[
            pltpu.VMEM(asks_shape, F32),
            pltpu.VMEM((n_recv, block, width), BF16),
            pltpu.VMEM((n_recv, block, width), BF16),
            pltpu.SemaphoreType.DMA((2, n_recv)),
            pltpu.SemaphoreType.DMA((2, n_recv)),
        ],
        compiler_params=pltpu.CompilerParams(
            collective_id=1, has_side_effects=True, vmem_limit_bytes=40 * 2**20
        ),
        name="fetch",
    )(wants, node_blocks)
    table = jnp.concatenate([node_blocks, got], axis=0)
    table_at = jnp.where(remote, nb_local + owners, send_blocks - base_block)

    frame_rows = frames.reshape(-1, 1, block)
    mask_rows = masks.reshape(slots, 1, block)
    edge_row = frame_edge.reshape(1, edge_width)
    recv_spec = pl.BlockSpec((block, width), lambda slot, local, *_: (local[slot], 0))
    sender_spec = pl.BlockSpec((1, block, width), lambda slot, local, at, *_: (at[slot], 0, 0))
    logit_shape = (slots, block, heads, block)
    sums_shape = (slots, block, 2 * heads, edge_width)
    slope_shape = (slots, block, block, edge_width)
    att_shape = (slots, block, att_width)
    stats_shape = (slots, 4, block * heads // 128, 128)
    weights = (w_query, w_key, w_value, w_left, w_right, edge_row, w_bias, w_edge_value, w_out)
    forward = pl.pallas_call(
        functools.partial(forward_kernel, scale),
        grid_spec=pltpu.PrefetchScalarGridSpec(
            num_scalar_prefetch=5,
            grid=(slots,),
            in_specs=[
                pl.BlockSpec((1, 1, block), lambda slot, local, at, recv, send, *_: (send[slot], 0, 0)),
                slot_spec(mask_rows.shape),
                recv_spec,
                recv_spec,
                sender_spec,
            ]
            + [whole_spec(weight) for weight in weights],
            out_specs=[
                slot_spec(shape)
                for shape in (
                    logit_shape, logit_shape, slope_shape, sums_shape, sums_shape, att_shape, stats_shape,
                )
            ],
            scratch_shapes=[
                pltpu.VMEM((block, edge_width), F32),
                pltpu.VMEM((block, block, edge_width), BF16),
                pltpu.VMEM((block * heads, block), BF16),
            ],
        ),
        out_shape=[
            jax.ShapeDtypeStruct(logit_shape, F32),
            jax.ShapeDtypeStruct(logit_shape, F32),
            jax.ShapeDtypeStruct(slope_shape, BF16),
            jax.ShapeDtypeStruct(sums_shape, BF16),
            jax.ShapeDtypeStruct(sums_shape, BF16),
            jax.ShapeDtypeStruct(att_shape, F32),
            jax.ShapeDtypeStruct(stats_shape, F32),
        ],
        compiler_params=pltpu.CompilerParams(vmem_limit_bytes=50 * 2**20),
        name="forward",
    )
    logits, dprobs, slopes, sums, wides, att_parts, stats = forward(
        local_blocks, table_at, pairs[0], send_blocks, frames,
        frame_rows, mask_rows, nodes, d_out, table, *weights,
    )

    joined_shape = (slots, 2) + stats.shape[2:]
    joined = pl.pallas_call(
        functools.partial(join_kernel, n_send),
        in_specs=[in_vmem],
        out_specs=in_vmem,
        out_shape=jax.ShapeDtypeStruct(joined_shape, F32),
        scratch_shapes=[
            pltpu.VMEM((n_send,) + stats.shape, F32),
            pltpu.SemaphoreType.DMA((2, n_send)),
        ],
        compiler_params=pltpu.CompilerParams(collective_id=2, has_side_effects=True),
        name="join",
    )(stats)

    weights = (w_query, w_key, w_value, w_left, w_right, w_out)
    node_shape = (nb_local, block, width)
    away_shape = (n_recv, block, width)
    att_sum_shape = (nb_local, block, att_width)
    backward = pl.pallas_call(
        functools.partial(backward_kernel, scale),
        grid_spec=pltpu.PrefetchScalarGridSpec(
            num_scalar_prefetch=2,
            grid=(slots,),
            in_specs=[slot_spec(mask_rows.shape), recv_spec, recv_spec, sender_spec]
            + [whole_spec(weight) for weight in weights]
            + [
                slot_spec(shape)
                for shape in (
                    logit_shape, logit_shape, slope_shape, sums_shape, sums_shape, att_shape, stats_shape,
                    joined.shape,
                )
            ],
            out_specs=[
                whole_spec(node_blocks),
                whole_spec(got),
                whole_spec(jax.ShapeDtypeStruct(att_sum_shape, F32)),
                whole_spec(w_edge_value),
                whole_spec(w_bias),
            ],
            scratch_shapes=[
                pltpu.VMEM((block * heads, block), BF16),
                pltpu.VMEM((block * heads, block), BF16),
                pltpu.VMEM((block * heads, edge_width), BF16),
                pltpu.VMEM((block, edge_width), F32),
                pltpu.VMEM((block, edge_width), F32),
            ],
        ),
        out_shape=[
            jax.ShapeDtypeStruct(node_shape, F32),
            jax.ShapeDtypeStruct(away_shape, BF16),
            jax.ShapeDtypeStruct(att_sum_shape, F32),
            jax.ShapeDtypeStruct(w_edge_value.shape, F32),
            jax.ShapeDtypeStruct(w_bias.shape, F32),
        ],
        compiler_params=pltpu.CompilerParams(vmem_limit_bytes=50 * 2**20),
        name="backward",
    )
    node_sum, leaving, att, grad_ev, grad_bias = backward(
        local_blocks, table_at, mask_rows, nodes, d_out, table, *weights,
        logits, dprobs, slopes, sums, wides, att_parts, stats, joined,
    )

    share = rows // n_send
    ev_share = edge_width // n_send
    bias_rows = heads * edge_width // att_width
    bias_flat = jnp.pad(grad_bias.reshape(bias_rows, att_width), ((0, 16 - bias_rows), (0, 0)))
    tail_rows = ev_share + 16
    mixed, grad_nodes, bias_flat, grad_ev = pl.pallas_call(
        functools.partial(tail_kernel, n_recv, n_send),
        in_specs=[in_vmem] * 9,
        out_specs=[in_vmem] * 4,
        out_shape=[
            jax.ShapeDtypeStruct((rows, width), BF16),
            jax.ShapeDtypeStruct((rows, width), F32),
            jax.ShapeDtypeStruct((16, att_width), F32),
            jax.ShapeDtypeStruct((edge_width, att_width), F32),
        ],
        scratch_shapes=[
            pltpu.VMEM(away_shape, BF16),
            pltpu.VMEM((n_send, share + tail_rows, att_width), BF16),
            pltpu.VMEM((n_send, share + tail_rows, att_width), BF16),
            pltpu.VMEM((n_send, share, width), BF16),
            pltpu.VMEM((n_recv, tail_rows, att_width), BF16),
            pltpu.VMEM((n_send, tail_rows, att_width), BF16),
            pltpu.VMEM((rows, width), F32),
            pltpu.VMEM((n_send, share, width), BF16),
            pltpu.VMEM((n_send, share, width), BF16),
            pltpu.VMEM((n_send, share, width), BF16),
            pltpu.SemaphoreType.DMA((2, n_recv)),
            pltpu.SemaphoreType.DMA((2, n_send)),
            pltpu.SemaphoreType.DMA((2, n_send)),
            pltpu.SemaphoreType.DMA((2, n_recv)),
            pltpu.SemaphoreType.DMA((2, n_send)),
            pltpu.SemaphoreType.DMA((2, n_send)),
            pltpu.SemaphoreType.DMA((2, n_send)),
        ],
        compiler_params=pltpu.CompilerParams(
            collective_id=3, has_side_effects=True, vmem_limit_bytes=40 * 2**20
        ),
        name="tail",
    )(att.reshape(rows, att_width), node_sum, leaving, asked, grad_ev, bias_flat, nodes, d_out, w_out)
    grad_bias = bias_flat[:bias_rows].reshape(heads, edge_width)
    return (mixed, grad_nodes, grad_bias, grad_ev)


def solution(mesh):
    in_specs = (
        P("recv", None),
        P(),
        P(None, ("recv", "send")),
        P(("recv", "send"), None),
        P("recv", None),
        P(),
        P(),
        P(),
        P(),
        P(),
        P(),
        P(),
        P(),
        P(),
    )
    out_specs = (P("recv", None), P("recv", None), P(), P())
    return jax.shard_map(body, mesh=mesh, in_specs=in_specs, out_specs=out_specs, check_vma=False)
```

```python
import functools

import jax
import jax.numpy as jnp
from jax import lax
from jax.experimental import pallas as pl
from jax.experimental.pallas import tpu as pltpu
from jax.sharding import PartitionSpec as P

NEG_LARGE = -1e30
CHUNK = 16
VMEM_LIMIT = 60 * 2**20
F32 = jnp.float32
BF16 = jnp.bfloat16


def dot(first, second, first_dim=1, second_dim=0):
    return lax.dot_general(
        first, second, (((first_dim,), (second_dim,)), ((), ())), preferred_element_type=F32
    )


def to_column(row):
    count = row.shape[1]
    eye = lax.broadcasted_iota(jnp.int32, (count, count), 0) == lax.broadcasted_iota(
        jnp.int32, (count, count), 1
    )
    return jnp.sum(jnp.where(eye, row, 0.0), axis=1, keepdims=True)


def to_row(column):
    count = column.shape[0]
    eye = lax.broadcasted_iota(jnp.int32, (count, count), 0) == lax.broadcasted_iota(
        jnp.int32, (count, count), 1
    )
    return jnp.sum(jnp.where(eye, column, 0.0), axis=0, keepdims=True)


def head_mask(heads, width):
    return lax.broadcasted_iota(jnp.int32, (heads, width), 1) // (
        width // heads
    ) == lax.broadcasted_iota(jnp.int32, (heads, width), 0)


def spread(rows, heads):
    count, width = rows.shape
    mask = head_mask(heads, width)
    wide = jnp.where(mask[None], rows.astype(F32)[:, None, :], 0.0)
    return wide.reshape(count * heads, width).astype(BF16)


def gather_heads(wide, heads):
    count, width = wide.shape
    mask = head_mask(heads, width)
    return jnp.sum(jnp.where(mask[None], wide.reshape(count // heads, heads, width), 0.0), axis=1)


def forward_kernel(
    scale,
    local_ref,
    table_ref,
    recv_ref,
    send_ref,
    frames_ref,
    frame_row_ref,
    mask_ref,
    nodes_ref,
    dout_ref,
    sender_ref,
    wq_ref,
    wk_ref,
    wv_ref,
    wl_ref,
    wr_ref,
    fe_ref,
    wb_ref,
    wev_ref,
    wo_ref,
    logit_ref,
    dprob_ref,
    slope_ref,
    sums_ref,
    wide_ref,
    att_ref,
    stats_ref,
    left_s,
    edge_s,
    probs_s,
):
    slot = pl.program_id(0)
    heads, edge_width = wb_ref.shape
    block = nodes_ref.shape[0]
    nodes = nodes_ref[...]
    sender = sender_ref[0]
    query = dot(nodes, wq_ref[...]).astype(BF16)
    left_s[...] = dot(nodes, wl_ref[...]) * 0.5
    datt = dot(dout_ref[...], wo_ref[...], 1, 1).astype(BF16)
    keys = dot(sender, wk_ref[...]).astype(BF16)
    values = dot(sender, wv_ref[...]).astype(BF16)
    right = dot(sender, wr_ref[...]) * 0.5
    right_same = (right + fe_ref[...].astype(F32) * 0.5).astype(BF16)
    right = right.astype(BF16)
    frame_col = jnp.broadcast_to(
        to_column(frame_row_ref[0].astype(F32)), (block, edge_width)
    ).astype(BF16)
    datt_wide = spread(datt, heads)
    logit_ref[0] = (dot(spread(query, heads), keys, 1, 1) * scale).reshape(block, heads, block)
    dprob_ref[0] = dot(datt_wide, values, 1, 1).reshape(block, heads, block)
    dctx = dot(datt_wide, wev_ref[...], 1, 1).reshape(block, heads, edge_width)
    bias = jnp.broadcast_to(wb_ref[...].astype(F32)[None], dctx.shape)
    wide_ref[0] = jnp.concatenate([bias, dctx], axis=1).astype(BF16)
    recv_start = recv_ref[slot] * block

    one = jnp.ones((), BF16)

    def edge_step(group, carry):
        start = group * CHUNK
        left_rows = left_s[pl.ds(start, CHUNK), :]
        for step in range(CHUNK):
            at = start + step
            frame = frames_ref[recv_start + at].astype(F32).astype(BF16)
            left = left_rows[step : step + 1].astype(BF16)
            half = left + jnp.where(frame_col == frame, right_same, right)
            turn = jnp.tanh(half)
            gain = half * turn
            edge = half + gain
            slope_ref[0, at] = (one + turn) * (one + (half - gain))
            edge_s[at] = edge
            both = dot(wide_ref[0, at], edge, 1, 1)
            logit_ref[0, at] = logit_ref[0, at] + both[:heads]
            dprob_ref[0, at] = dprob_ref[0, at] + both[heads:]
        return carry

    lax.fori_loop(0, block // CHUNK, edge_step, 0)
    valid = mask_ref[0] > 0

    def soft_step(group, carry):
        start = group * CHUNK
        rows = pl.ds(start * heads, CHUNK * heads)
        logits = logit_ref[0, pl.ds(start, CHUNK)].reshape(CHUNK * heads, block)
        dprob = dprob_ref[0, pl.ds(start, CHUNK)].reshape(CHUNK * heads, block)
        logits = jnp.where(valid, logits, NEG_LARGE)
        top = jnp.max(logits, axis=1, keepdims=True)
        probs = jnp.where(valid, jnp.exp(logits - top), 0.0)
        weighted = probs * dprob
        stats_ref[0, 0, pl.ds(group, 1), :] = to_row(top)
        stats_ref[0, 1, pl.ds(group, 1), :] = to_row(jnp.sum(probs, axis=1, keepdims=True))
        stats_ref[0, 2, pl.ds(group, 1), :] = to_row(jnp.sum(weighted, axis=1, keepdims=True))
        probs_s[rows, :] = probs.astype(BF16)
        pair = jnp.concatenate(
            [probs.reshape(CHUNK, heads, block), weighted.reshape(CHUNK, heads, block)], axis=1
        ).astype(BF16)
        for step in range(CHUNK):
            at = start + step
            sums_ref[0, at] = dot(pair[step], edge_s[at]).astype(BF16)
        return carry

    lax.fori_loop(0, block // CHUNK, soft_step, 0)
    stats_ref[0, 3] = jnp.full(stats_ref.shape[2:], local_ref[slot].astype(F32), F32)
    ctx = sums_ref[0].astype(F32)[:, :heads].reshape(block * heads, edge_width).astype(BF16)
    att_ref[0] = gather_heads(dot(probs_s[...], values) + dot(ctx, wev_ref[...]), heads)


def backward_kernel(
    scale,
    local_ref,
    table_ref,
    mask_ref,
    nodes_ref,
    dout_ref,
    sender_ref,
    wq_ref,
    wk_ref,
    wv_ref,
    wl_ref,
    wr_ref,
    wo_ref,
    logit_ref,
    dprob_ref,
    slope_ref,
    sums_ref,
    wide_ref,
    att_in_ref,
    stats_ref,
    joined_ref,
    node_ref,
    leaving_ref,
    att_ref,
    grad_ev_ref,
    grad_bias_ref,
    probs_s,
    dlogit_s,
    ctx_s,
    left_s,
    right_s,
):
    slot = pl.program_id(0)
    heads = logit_ref.shape[2]
    block = nodes_ref.shape[0]
    edge_width = wide_ref.shape[3]
    width = wq_ref.shape[1]
    mask = head_mask(heads, width)
    valid = mask_ref[0] > 0

    @pl.when(slot == 0)
    def _():
        grad_ev_ref[...] = jnp.zeros_like(grad_ev_ref)
        grad_bias_ref[...] = jnp.zeros_like(grad_bias_ref)
        node_ref[...] = jnp.zeros_like(node_ref)
        leaving_ref[...] = jnp.zeros_like(leaving_ref)
        att_ref[...] = jnp.zeros_like(att_ref)

    local = local_ref[slot]
    place = table_ref[slot]
    own_blocks = node_ref.shape[0]
    right_s[...] = jnp.zeros_like(right_s)

    def step_group(group, carry):
        start = group * CHUNK
        rows = pl.ds(start * heads, CHUNK * heads)
        lse = joined_ref[0, 0, pl.ds(group, 1), :]
        lse_col = to_column(lse)
        delta_col = to_column(joined_ref[0, 1, pl.ds(group, 1), :])
        factor_col = to_column(jnp.exp(stats_ref[0, 0, pl.ds(group, 1), :] - lse))
        logits = logit_ref[0, pl.ds(start, CHUNK)].reshape(CHUNK * heads, block)
        dprob = dprob_ref[0, pl.ds(start, CHUNK)].reshape(CHUNK * heads, block)
        probs = jnp.where(valid, jnp.exp(logits - lse_col), 0.0)
        dlogit = probs * (dprob - delta_col)
        probs_s[rows, :] = probs.astype(BF16)
        dlogit_s[rows, :] = dlogit.astype(BF16)
        sums = sums_ref[0, pl.ds(start, CHUNK)].astype(F32)
        ctx = sums[:, :heads].reshape(CHUNK * heads, edge_width) * factor_col
        ctx_s[rows, :] = ctx.astype(BF16)
        moved = sums[:, heads:].reshape(CHUNK * heads, edge_width) * factor_col - ctx * delta_col
        grad_bias_ref[...] += jnp.sum(moved.reshape(CHUNK, heads, edge_width), axis=0)
        factor = jnp.sum(
            jnp.where(mask[None], factor_col.reshape(CHUNK, heads, 1), 0.0), axis=1
        )
        att_ref[local, pl.ds(start, CHUNK), :] += att_in_ref[0, pl.ds(start, CHUNK), :] * factor
        pair = jnp.concatenate(
            [dlogit.reshape(CHUNK, heads, block), probs.reshape(CHUNK, heads, block)], axis=1
        ).astype(BF16)
        right_sum = right_s[...]
        lefts = []
        for step in range(CHUNK):
            at = start + step
            d_edge = dot(pair[step], wide_ref[0, at], 0, 0)
            d_pre = d_edge * slope_ref[0, at].astype(F32)
            right_sum = right_sum + d_pre
            lefts.append(jnp.sum(d_pre, axis=0, keepdims=True))
        right_s[...] = right_sum
        left_s[pl.ds(start, CHUNK), :] = jnp.concatenate(lefts, axis=0)
        return carry

    lax.fori_loop(0, block // CHUNK, step_group, 0)
    nodes = nodes_ref[...]
    sender = sender_ref[0]
    query_wide = spread(dot(nodes, wq_ref[...]).astype(BF16), heads)
    datt_wide = spread(dot(dout_ref[...], wo_ref[...], 1, 1).astype(BF16), heads)
    keys = dot(sender, wk_ref[...]).astype(BF16)
    dlogit = dlogit_s[...]
    grad_query = gather_heads(dot(dlogit, keys), heads) * scale
    grad_keys = dot(dlogit, query_wide, 0, 0) * scale
    grad_values = dot(probs_s[...], datt_wide, 0, 0)
    node_ref[local] += dot(grad_query.astype(BF16), wq_ref[...], 1, 1) + 0.5 * dot(
        left_s[...].astype(BF16), wl_ref[...], 1, 1
    )
    send_grad = (
        dot(grad_keys.astype(BF16), wk_ref[...], 1, 1)
        + dot(grad_values.astype(BF16), wv_ref[...], 1, 1)
        + 0.5 * dot(right_s[...].astype(BF16), wr_ref[...], 1, 1)
    )

    @pl.when(place < own_blocks)
    def _():
        node_ref[place] += send_grad

    @pl.when(place >= own_blocks)
    def _():
        leaving_ref[place - own_blocks] = send_grad.astype(BF16)

    grad_ev_ref[...] += dot(ctx_s[...], datt_wide, 0, 0)


MESH = pl.DeviceIdType.MESH


def peers_of(axis, count):
    me = lax.axis_index(axis)
    return me, [
        (offset, lax.rem(me + offset, count), lax.rem(me + count - offset, count))
        for offset in range(1, count)
    ]


def meet(groups):
    barrier = pltpu.get_barrier_semaphore()
    total = 0
    for axis, peers in groups:
        for _, target, _ in peers:
            pl.semaphore_signal(barrier, inc=1, device_id={axis: target}, device_id_type=MESH)
            total += 1
    pl.semaphore_wait(barrier, total)


def post(axis, peers, sems, source, landing):
    copies = []
    for offset, target, _ in peers:
        copy = pltpu.make_async_remote_copy(
            src_ref=source(target),
            dst_ref=landing,
            send_sem=sems.at[0, offset],
            recv_sem=sems.at[1, offset],
            device_id={axis: target},
            device_id_type=MESH,
        )
        copy.start()
        copies.append(copy)
    return copies


def fetch_kernel(
    n_recv, pairs_ref, nodes_ref, got_ref, asked_ref, want_s, ask_s, reply_s, got_s, ask_sems, reply_sems
):
    me, peers = peers_of("recv", n_recv)
    blocks = nodes_ref.shape[0]
    for _, target, _ in peers:
        wanted = 0
        for slot in range(pairs_ref.shape[1]):
            sender = pairs_ref[1, slot]
            wanted = wanted + jnp.where(sender // blocks == target, sender % blocks, 0)
        want_s[target] = jnp.full(want_s.shape[1:], wanted, jnp.int32).astype(F32)
    meet([("recv", peers)])
    asks = post("recv", peers, ask_sems, lambda target: want_s.at[target], ask_s.at[me])
    nodes = nodes_ref[...].astype(F32)
    for copy in asks:
        copy.wait_recv()
    replies = []
    for peer in peers:
        offset, target, _ = peer
        ask = ask_s[target][0:1, 0:1]
        reply = nodes[0]
        for at in range(1, nodes.shape[0]):
            reply = jnp.where(ask == float(at), nodes[at], reply)
        reply_s[offset] = reply.astype(BF16)
        replies += post("recv", [peer], reply_sems, lambda target: reply_s.at[offset], got_s.at[me])
    asked_ref[...] = jnp.zeros_like(asked_ref)
    got_ref[...] = jnp.zeros_like(got_ref)
    for _, target, _ in peers:
        asked_ref[target] = ask_s[target]
    for copy, (_, _, source) in zip(replies, peers):
        copy.wait_recv()
        got_ref[source] = got_s[source]
    for copy in asks + replies:
        copy.wait_send()


def join_kernel(n_send, stats_ref, joined_ref, all_s, sems):
    me, peers = peers_of("send", n_send)
    meet([("send", peers)])
    copies = post("send", peers, sems, lambda target: stats_ref, all_s.at[me])
    slots = stats_ref.shape[0]
    all_s[me] = stats_ref[...]
    for copy in copies:
        copy.wait_recv()
    for slot in range(slots):
        lands = stats_ref[slot, 3]
        top = stats_ref[slot, 0]
        for device in range(n_send):
            for other in range(slots):
                top = jnp.maximum(
                    top,
                    jnp.where(all_s[device, other, 3] == lands, all_s[device, other, 0], NEG_LARGE),
                )
        total = jnp.zeros_like(top)
        delta = jnp.zeros_like(top)
        for device in range(n_send):
            for other in range(slots):
                part = jnp.where(
                    all_s[device, other, 3] == lands, jnp.exp(all_s[device, other, 0] - top), 0.0
                )
                total = total + part * all_s[device, other, 1]
                delta = delta + part * all_s[device, other, 2]
        joined_ref[slot, 0] = top + jnp.log(total)
        joined_ref[slot, 1] = delta / total
    for copy in copies:
        copy.wait_send()


def tail_kernel(
    n_recv,
    n_send,
    att_ref,
    node_ref,
    leaving_ref,
    asked_ref,
    ev_ref,
    bias_ref,
    nodes_ref,
    dout_ref,
    wo_ref,
    mixed_ref,
    grad_ref,
    bias_out_ref,
    ev_out_ref,
    back_s,
    out_a,
    in_a,
    mix_s,
    small_s,
    small_all,
    acc_s,
    out_n,
    in_n,
    fin_s,
    back_sems,
    a_sems,
    mix_sems,
    small_sems,
    small_all_sems,
    n_sems,
    fin_sems,
):
    row, row_peers = peers_of("recv", n_recv)
    col, col_peers = peers_of("send", n_send)
    blocks, block, width = node_ref.shape
    rows = blocks * block
    share = rows // n_send
    ev_share = ev_ref.shape[0] // n_send
    bias_rows = bias_ref.shape[0]
    meet([("recv", row_peers), ("send", col_peers)])
    backs = post("recv", row_peers, back_sems, lambda target: leaving_ref.at[target], back_s.at[row])
    for part in range(n_send):
        out_a[part, :share] = att_ref[part * share : (part + 1) * share].astype(BF16)
        out_a[part, share : share + ev_share] = ev_ref[
            part * ev_share : (part + 1) * ev_share
        ].astype(BF16)
        bias = bias_ref[...] if part == 0 else jnp.zeros_like(bias_ref)
        out_a[part, share + ev_share :] = bias.astype(BF16)
    sent_a = post("send", col_peers, a_sems, lambda target: out_a.at[target], in_a.at[col])
    acc_s[...] = node_ref[...].reshape(rows, width)
    total = out_a[col].astype(F32)
    for copy, (_, _, source) in zip(sent_a, col_peers):
        copy.wait_recv()
        total = total + in_a[source].astype(F32)
    small_s[row] = total[share:].astype(BF16)
    smalls = post("recv", row_peers, small_sems, lambda target: small_s.at[row], small_s.at[row])
    here = pl.ds(pl.multiple_of(col * share, share), share)
    mixed = nodes_ref[here, :].astype(F32) + dot(total[:share].astype(BF16), wo_ref[...])
    mix_s[col] = mixed.astype(BF16)
    mixes = post("send", col_peers, mix_sems, lambda target: mix_s.at[col], mix_s.at[col])
    for copy, (_, _, source) in zip(backs, row_peers):
        copy.wait_recv()
        asked = asked_ref[source][0:1, 0:1]
        landed = back_s[source].astype(F32)
        for at in range(blocks):
            acc_s[at * block : (at + 1) * block, :] += jnp.where(asked == float(at), landed, 0.0)
    for part in range(n_send):
        out_n[part] = acc_s[part * share : (part + 1) * share, :].astype(BF16)
    sent_n = post("send", col_peers, n_sems, lambda target: out_n.at[target], in_n.at[col])
    for copy in smalls:
        copy.wait_recv()
    small = small_s[0].astype(F32)
    for at in range(1, n_recv):
        small = small + small_s[at].astype(F32)
    small_all[col] = small.astype(BF16)
    small_alls = post(
        "send", col_peers, small_all_sems, lambda target: small_all.at[col], small_all.at[col]
    )
    total = out_n[col].astype(F32)
    for copy, (_, _, source) in zip(sent_n, col_peers):
        copy.wait_recv()
        total = total + in_n[source].astype(F32)
    fin_s[col] = total.astype(BF16)
    fins = post("send", col_peers, fin_sems, lambda target: fin_s.at[col], fin_s.at[col])
    for copy in mixes:
        copy.wait_recv()
    mixed_ref[...] = mix_s[...].reshape(rows, width)
    for copy in small_alls:
        copy.wait_recv()
    for part in range(n_send):
        ev_out_ref[part * ev_share : (part + 1) * ev_share, :] = small_all[part, :ev_share].astype(F32)
    bias_out_ref[...] = small_all[0, ev_share : ev_share + bias_rows].astype(F32)
    for copy in fins:
        copy.wait_recv()
    for part in range(n_send):
        span = slice(part * share, (part + 1) * share)
        grad_ref[span, :] = dout_ref[span, :].astype(F32) + fin_s[part].astype(F32)
    for copy in backs + sent_a + smalls + mixes + sent_n + small_alls + fins:
        copy.wait_send()


def whole_spec(array):
    zeros = (0,) * array.ndim
    return pl.BlockSpec(array.shape, lambda slot, *_: zeros)


def slot_spec(shape):
    rest = (0,) * (len(shape) - 1)
    return pl.BlockSpec((1,) + tuple(shape[1:]), lambda slot, *_: (slot,) + rest)


def body(
    nodes,
    frames,
    pairs,
    masks,
    d_out,
    w_query,
    w_key,
    w_value,
    w_left,
    w_right,
    frame_edge,
    w_bias,
    w_edge_value,
    w_out,
):
    rows, width = nodes.shape
    slots, block = masks.shape
    nb_local = rows // block
    heads, edge_width = w_bias.shape
    att_width = w_query.shape[1]
    scale = (att_width // heads) ** (-0.5)
    my_recv = lax.axis_index("recv")
    n_recv = lax.axis_size("recv")
    n_send = lax.axis_size("send")
    base_block = my_recv * nb_local

    send_blocks = pairs[1]
    local_blocks = pairs[0] - base_block
    owners = send_blocks // nb_local
    remote = owners != my_recv
    owner_ids = jnp.arange(n_recv, dtype=jnp.int32)
    node_blocks = nodes.reshape(nb_local, block, width)
    in_vmem = pl.BlockSpec(memory_space=pltpu.VMEM)
    asks_shape = (n_recv, 8, 128)
    got, asked = pl.pallas_call(
        functools.partial(fetch_kernel, n_recv),
        in_specs=[pl.BlockSpec(memory_space=pltpu.SMEM), in_vmem],
        out_specs=[in_vmem] * 2,
        out_shape=[
            jax.ShapeDtypeStruct((n_recv, block, width), BF16),
            jax.ShapeDtypeStruct(asks_shape, F32),
        ],
        scratch_shapes=[
            pltpu.VMEM(asks_shape, F32),
            pltpu.VMEM(asks_shape, F32),
            pltpu.VMEM((n_recv, block, width), BF16),
            pltpu.VMEM((n_recv, block, width), BF16),
            pltpu.SemaphoreType.DMA((2, n_recv)),
            pltpu.SemaphoreType.DMA((2, n_recv)),
        ],
        compiler_params=pltpu.CompilerParams(
            collective_id=1, has_side_effects=True, vmem_limit_bytes=VMEM_LIMIT
        ),
        name="fetch",
    )(pairs, node_blocks)
    table = jnp.concatenate([node_blocks, got], axis=0)
    table_at = jnp.where(remote, nb_local + owners, send_blocks - base_block)

    frame_rows = frames.reshape(-1, 1, block)
    mask_rows = masks.reshape(slots, 1, block)
    edge_row = frame_edge.reshape(1, edge_width)
    recv_spec = pl.BlockSpec((block, width), lambda slot, local, *_: (local[slot], 0))
    sender_spec = pl.BlockSpec((1, block, width), lambda slot, local, at, *_: (at[slot], 0, 0))
    logit_shape = (slots, block, heads, block)
    sums_shape = (slots, block, 2 * heads, edge_width)
    slope_shape = (slots, block, block, edge_width)
    att_shape = (slots, block, att_width)
    stats_shape = (slots, 4, block * heads // 128, 128)
    weights = (w_query, w_key, w_value, w_left, w_right, edge_row, w_bias, w_edge_value, w_out)
    forward = pl.pallas_call(
        functools.partial(forward_kernel, scale),
        grid_spec=pltpu.PrefetchScalarGridSpec(
            num_scalar_prefetch=5,
            grid=(slots,),
            in_specs=[
                pl.BlockSpec((1, 1, block), lambda slot, local, at, recv, send, *_: (send[slot], 0, 0)),
                slot_spec(mask_rows.shape),
                recv_spec,
                recv_spec,
                sender_spec,
            ]
            + [whole_spec(weight) for weight in weights],
            out_specs=[
                slot_spec(shape)
                for shape in (
                    logit_shape, logit_shape, slope_shape, sums_shape, sums_shape, att_shape, stats_shape,
                )
            ],
            scratch_shapes=[
                pltpu.VMEM((block, edge_width), F32),
                pltpu.VMEM((block, block, edge_width), BF16),
                pltpu.VMEM((block * heads, block), BF16),
            ],
        ),
        out_shape=[
            jax.ShapeDtypeStruct(logit_shape, F32),
            jax.ShapeDtypeStruct(logit_shape, F32),
            jax.ShapeDtypeStruct(slope_shape, BF16),
            jax.ShapeDtypeStruct(sums_shape, BF16),
            jax.ShapeDtypeStruct(sums_shape, BF16),
            jax.ShapeDtypeStruct(att_shape, F32),
            jax.ShapeDtypeStruct(stats_shape, F32),
        ],
        compiler_params=pltpu.CompilerParams(vmem_limit_bytes=VMEM_LIMIT),
        name="forward",
    )
    logits, dprobs, slopes, sums, wides, att_parts, stats = forward(
        local_blocks, table_at, pairs[0], send_blocks, frames,
        frame_rows, mask_rows, nodes, d_out, table, *weights,
    )

    joined_shape = (slots, 2) + stats.shape[2:]
    joined = pl.pallas_call(
        functools.partial(join_kernel, n_send),
        in_specs=[in_vmem],
        out_specs=in_vmem,
        out_shape=jax.ShapeDtypeStruct(joined_shape, F32),
        scratch_shapes=[
            pltpu.VMEM((n_send,) + stats.shape, F32),
            pltpu.SemaphoreType.DMA((2, n_send)),
        ],
        compiler_params=pltpu.CompilerParams(
            collective_id=2, has_side_effects=True, vmem_limit_bytes=VMEM_LIMIT
        ),
        name="join",
    )(stats)

    weights = (w_query, w_key, w_value, w_left, w_right, w_out)
    node_shape = (nb_local, block, width)
    away_shape = (n_recv, block, width)
    att_sum_shape = (nb_local, block, att_width)
    backward = pl.pallas_call(
        functools.partial(backward_kernel, scale),
        grid_spec=pltpu.PrefetchScalarGridSpec(
            num_scalar_prefetch=2,
            grid=(slots,),
            in_specs=[slot_spec(mask_rows.shape), recv_spec, recv_spec, sender_spec]
            + [whole_spec(weight) for weight in weights]
            + [
                slot_spec(shape)
                for shape in (
                    logit_shape, logit_shape, slope_shape, sums_shape, sums_shape, att_shape, stats_shape,
                    joined.shape,
                )
            ],
            out_specs=[
                whole_spec(node_blocks),
                whole_spec(got),
                whole_spec(jax.ShapeDtypeStruct(att_sum_shape, F32)),
                whole_spec(w_edge_value),
                whole_spec(w_bias),
            ],
            scratch_shapes=[
                pltpu.VMEM((block * heads, block), BF16),
                pltpu.VMEM((block * heads, block), BF16),
                pltpu.VMEM((block * heads, edge_width), BF16),
                pltpu.VMEM((block, edge_width), F32),
                pltpu.VMEM((block, edge_width), F32),
            ],
        ),
        out_shape=[
            jax.ShapeDtypeStruct(node_shape, F32),
            jax.ShapeDtypeStruct(away_shape, BF16),
            jax.ShapeDtypeStruct(att_sum_shape, F32),
            jax.ShapeDtypeStruct(w_edge_value.shape, F32),
            jax.ShapeDtypeStruct(w_bias.shape, F32),
        ],
        compiler_params=pltpu.CompilerParams(vmem_limit_bytes=VMEM_LIMIT),
        name="backward",
    )
    node_sum, leaving, att, grad_ev, grad_bias = backward(
        local_blocks, table_at, mask_rows, nodes, d_out, table, *weights,
        logits, dprobs, slopes, sums, wides, att_parts, stats, joined,
    )

    share = rows // n_send
    ev_share = edge_width // n_send
    bias_rows = heads * edge_width // att_width
    bias_flat = jnp.pad(grad_bias.reshape(bias_rows, att_width), ((0, 16 - bias_rows), (0, 0)))
    tail_rows = ev_share + 16
    mixed, grad_nodes, bias_flat, grad_ev = pl.pallas_call(
        functools.partial(tail_kernel, n_recv, n_send),
        in_specs=[in_vmem] * 9,
        out_specs=[in_vmem] * 4,
        out_shape=[
            jax.ShapeDtypeStruct((rows, width), BF16),
            jax.ShapeDtypeStruct((rows, width), F32),
            jax.ShapeDtypeStruct((16, att_width), F32),
            jax.ShapeDtypeStruct((edge_width, att_width), F32),
        ],
        scratch_shapes=[
            pltpu.VMEM(away_shape, BF16),
            pltpu.VMEM((n_send, share + tail_rows, att_width), BF16),
            pltpu.VMEM((n_send, share + tail_rows, att_width), BF16),
            pltpu.VMEM((n_send, share, width), BF16),
            pltpu.VMEM((n_recv, tail_rows, att_width), BF16),
            pltpu.VMEM((n_send, tail_rows, att_width), BF16),
            pltpu.VMEM((rows, width), F32),
            pltpu.VMEM((n_send, share, width), BF16),
            pltpu.VMEM((n_send, share, width), BF16),
            pltpu.VMEM((n_send, share, width), BF16),
            pltpu.SemaphoreType.DMA((2, n_recv)),
            pltpu.SemaphoreType.DMA((2, n_send)),
            pltpu.SemaphoreType.DMA((2, n_send)),
            pltpu.SemaphoreType.DMA((2, n_recv)),
            pltpu.SemaphoreType.DMA((2, n_send)),
            pltpu.SemaphoreType.DMA((2, n_send)),
            pltpu.SemaphoreType.DMA((2, n_send)),
        ],
        compiler_params=pltpu.CompilerParams(
            collective_id=3, has_side_effects=True, vmem_limit_bytes=VMEM_LIMIT
        ),
        name="tail",
    )(att.reshape(rows, att_width), node_sum, leaving, asked, grad_ev, bias_flat, nodes, d_out, w_out)
    grad_bias = bias_flat[:bias_rows].reshape(heads, edge_width)
    return (mixed, grad_nodes, grad_bias, grad_ev)


def solution(mesh):
    in_specs = (
        P("recv", None),
        P(),
        P(None, ("recv", "send")),
        P(("recv", "send"), None),
        P("recv", None),
        P(),
        P(),
        P(),
        P(),
        P(),
        P(),
        P(),
        P(),
        P(),
    )
    out_specs = (P("recv", None), P("recv", None), P(), P())
    return jax.shard_map(body, mesh=mesh, in_specs=in_specs, out_specs=out_specs, check_vma=False)
```

```python
import functools

import jax
import jax.numpy as jnp
from jax import lax
from jax.experimental import pallas as pl
from jax.experimental.pallas import tpu as pltpu
from jax.sharding import PartitionSpec as P

NEG_LARGE = -1e30
CHUNK = 16
GROUP = 8
BIAS_ROWS = 16
VMEM_LIMIT = 60 * 2**20
TAIL_LIMIT = 32 * 2**20
F32 = jnp.float32
BF16 = jnp.bfloat16


def dot(first, second, first_dim=1, second_dim=0):
    return lax.dot_general(
        first, second, (((first_dim,), (second_dim,)), ((), ())), preferred_element_type=F32
    )


def to_column(row):
    count = row.shape[1]
    eye = lax.broadcasted_iota(jnp.int32, (count, count), 0) == lax.broadcasted_iota(
        jnp.int32, (count, count), 1
    )
    return jnp.sum(jnp.where(eye, row, 0.0), axis=1, keepdims=True)


def to_row(column):
    count = column.shape[0]
    eye = lax.broadcasted_iota(jnp.int32, (count, count), 0) == lax.broadcasted_iota(
        jnp.int32, (count, count), 1
    )
    return jnp.sum(jnp.where(eye, column, 0.0), axis=0, keepdims=True)


def head_mask(heads, width):
    return lax.broadcasted_iota(jnp.int32, (heads, width), 1) // (
        width // heads
    ) == lax.broadcasted_iota(jnp.int32, (heads, width), 0)


def spread(rows, heads):
    count, width = rows.shape
    mask = head_mask(heads, width)
    wide = jnp.where(mask[None], rows.astype(F32)[:, None, :], 0.0)
    return wide.reshape(count * heads, width).astype(BF16)


def gather_heads(wide, heads):
    count, width = wide.shape
    mask = head_mask(heads, width)
    return jnp.sum(jnp.where(mask[None], wide.reshape(count // heads, heads, width), 0.0), axis=1)


def forward_kernel(
    scale,
    own_blocks,
    pairs_ref,
    frames_ref,
    frame_row_ref,
    mask_ref,
    nodes_ref,
    dout_ref,
    sender_ref,
    wq_ref,
    wk_ref,
    wv_ref,
    wl_ref,
    wr_ref,
    fe_ref,
    wb_ref,
    wev_ref,
    wo_ref,
    logit_ref,
    dprob_ref,
    slope_ref,
    sums_ref,
    wide_ref,
    att_ref,
    stats_ref,
    left_s,
    edge_s,
    probs_s,
):
    slot = pl.program_id(0)
    heads, edge_width = wb_ref.shape
    block = nodes_ref.shape[0]
    nodes = nodes_ref[...]
    sender = sender_ref[0]
    query = dot(nodes, wq_ref[...]).astype(BF16)
    left_s[...] = dot(nodes, wl_ref[...]) * 0.5
    datt = dot(dout_ref[...], wo_ref[...], 1, 1).astype(BF16)
    keys = dot(sender, wk_ref[...]).astype(BF16)
    values = dot(sender, wv_ref[...]).astype(BF16)
    right = dot(sender, wr_ref[...]) * 0.5
    right_same = (right + fe_ref[...].astype(F32) * 0.5).astype(BF16)
    right = right.astype(BF16)
    frame_col = jnp.broadcast_to(
        to_column(frame_row_ref[0].astype(F32)), (block, edge_width)
    ).astype(BF16)
    datt_wide = spread(datt, heads)
    logit_ref[0] = (dot(spread(query, heads), keys, 1, 1) * scale).reshape(block, heads, block)
    dprob_ref[0] = dot(datt_wide, values, 1, 1).reshape(block, heads, block)
    dctx = dot(datt_wide, wev_ref[...], 1, 1).reshape(block, heads, edge_width)
    bias = jnp.broadcast_to(wb_ref[...].astype(F32)[None], dctx.shape)
    wide_ref[0] = jnp.concatenate([bias, dctx], axis=1).astype(BF16)
    recv_start = pairs_ref[0, slot] * block

    one = jnp.ones((), BF16)

    def edge_step(group, carry):
        start = group * CHUNK
        left_rows = left_s[pl.ds(start, CHUNK), :].astype(BF16)
        for step in range(0, CHUNK, 2):
            edges = []
            for at in (step, step + 1):
                frame = frames_ref[recv_start + start + at].astype(F32).astype(BF16)
                half = left_rows[at : at + 1] + jnp.where(frame_col == frame, right_same, right)
                turn = jnp.tanh(half)
                gain = half * turn
                edge = half + gain
                slope_ref[0, start + at] = (one + turn) * (one + (half - gain))
                edge_s[start + at] = edge
                edges.append(edge)
            wide = wide_ref[0, pl.ds(start + step, 2)].reshape(4 * heads, edge_width)
            both = dot(wide, jnp.concatenate(edges, axis=0), 1, 1)
            for at in (0, 1):
                part = both[2 * heads * at : 2 * heads * (at + 1), block * at : block * (at + 1)]
                here = start + step + at
                logit_ref[0, here] = logit_ref[0, here] + part[:heads]
                dprob_ref[0, here] = dprob_ref[0, here] + part[heads:]
        return carry

    lax.fori_loop(0, block // CHUNK, edge_step, 0)
    valid = mask_ref[0] > 0

    def soft_step(group, carry):
        start = group * CHUNK
        rows = pl.ds(start * heads, CHUNK * heads)
        logits = logit_ref[0, pl.ds(start, CHUNK)].reshape(CHUNK * heads, block)
        dprob = dprob_ref[0, pl.ds(start, CHUNK)].reshape(CHUNK * heads, block)
        logits = jnp.where(valid, logits, NEG_LARGE)
        top = jnp.max(logits, axis=1, keepdims=True)
        probs = jnp.where(valid, jnp.exp(logits - top), 0.0)
        weighted = probs * dprob
        stats_ref[0, 0, pl.ds(group, 1), :] = to_row(top)
        stats_ref[0, 1, pl.ds(group, 1), :] = to_row(jnp.sum(probs, axis=1, keepdims=True))
        stats_ref[0, 2, pl.ds(group, 1), :] = to_row(jnp.sum(weighted, axis=1, keepdims=True))
        probs_s[rows, :] = probs.astype(BF16)
        pair = jnp.concatenate(
            [probs.reshape(CHUNK, heads, block), weighted.reshape(CHUNK, heads, block)], axis=1
        ).astype(BF16)
        for step in range(0, CHUNK, 2):
            edges = jnp.concatenate([edge_s[start + step], edge_s[start + step + 1]], axis=1)
            both = dot(pair[step : step + 2].reshape(4 * heads, block), edges).astype(BF16)
            sums_ref[0, start + step] = both[: 2 * heads, :edge_width]
            sums_ref[0, start + step + 1] = both[2 * heads :, edge_width:]
        return carry

    lax.fori_loop(0, block // CHUNK, soft_step, 0)
    stats_ref[0, 3] = jnp.full(stats_ref.shape[2:], pairs_ref[0, slot].astype(F32), F32)
    ctx = sums_ref[0].astype(F32)[:, :heads].reshape(block * heads, edge_width).astype(BF16)
    att_ref[0] = gather_heads(dot(probs_s[...], values) + dot(ctx, wev_ref[...]), heads)


def backward_kernel(
    scale,
    own_blocks,
    pairs_ref,
    mask_ref,
    nodes_ref,
    dout_ref,
    sender_ref,
    wq_ref,
    wk_ref,
    wv_ref,
    wl_ref,
    wr_ref,
    wo_ref,
    logit_ref,
    dprob_ref,
    slope_ref,
    sums_ref,
    wide_ref,
    att_in_ref,
    stats_ref,
    joined_ref,
    node_ref,
    leaving_ref,
    att_ref,
    grad_ev_ref,
    grad_bias_ref,
    probs_s,
    dlogit_s,
    ctx_s,
    left_s,
    right_s,
    diagonal_s,
):
    slot = pl.program_id(0)
    heads = logit_ref.shape[2]
    block = nodes_ref.shape[0]
    edge_width = wide_ref.shape[3]
    width = wq_ref.shape[1]
    mask = head_mask(heads, width)
    valid = mask_ref[0] > 0

    @pl.when(slot == 0)
    def _():
        grad_ev_ref[...] = jnp.zeros_like(grad_ev_ref)
        grad_bias_ref[...] = jnp.zeros_like(grad_bias_ref)
        node_ref[...] = jnp.zeros_like(node_ref)
        diagonal_s[...] = jnp.zeros_like(diagonal_s)
        leaving_ref[...] = jnp.zeros_like(leaving_ref)
        att_ref[...] = jnp.zeros_like(att_ref)

    local = pairs_ref[0, slot] % own_blocks
    place = table_place(own_blocks, slot, pairs_ref)
    right_s[...] = jnp.zeros_like(right_s)

    def step_group(group, carry):
        start = group * CHUNK
        rows = pl.ds(start * heads, CHUNK * heads)
        lse = joined_ref[0, 0, pl.ds(group, 1), :]
        lse_col = to_column(lse)
        delta_col = to_column(joined_ref[0, 1, pl.ds(group, 1), :])
        factor_col = to_column(jnp.exp(stats_ref[0, 0, pl.ds(group, 1), :] - lse))
        logits = logit_ref[0, pl.ds(start, CHUNK)].reshape(CHUNK * heads, block)
        dprob = dprob_ref[0, pl.ds(start, CHUNK)].reshape(CHUNK * heads, block)
        probs = jnp.where(valid, jnp.exp(logits - lse_col), 0.0)
        dlogit = probs * (dprob - delta_col)
        probs_s[rows, :] = probs.astype(BF16)
        dlogit_s[rows, :] = dlogit.astype(BF16)
        sums = sums_ref[0, pl.ds(start, CHUNK)].astype(F32)
        ctx = sums[:, :heads].reshape(CHUNK * heads, edge_width) * factor_col
        ctx_s[rows, :] = ctx.astype(BF16)
        moved = sums[:, heads:].reshape(CHUNK * heads, edge_width) * factor_col - ctx * delta_col
        grad_bias_ref[...] += jnp.sum(moved.reshape(CHUNK, heads, edge_width), axis=0)
        factor = jnp.sum(
            jnp.where(mask[None], factor_col.reshape(CHUNK, heads, 1), 0.0), axis=1
        )
        att_ref[local, pl.ds(start, CHUNK), :] += att_in_ref[0, pl.ds(start, CHUNK), :] * factor
        pair = jnp.concatenate(
            [dlogit.reshape(CHUNK, heads, block), probs.reshape(CHUNK, heads, block)], axis=1
        ).astype(BF16)
        right_sum = right_s[...]
        lefts = []
        for half in range(CHUNK // GROUP):
            first = half * GROUP
            for step in range(GROUP):
                diagonal_s[
                    half,
                    2 * heads * step : 2 * heads * (step + 1),
                    edge_width * step : edge_width * (step + 1),
                ] = wide_ref[0, start + first + step]
            pairs = pair[first : first + GROUP].reshape(GROUP * 2 * heads, block)
            d_edges = dot(pairs, diagonal_s[half], 0, 0)
            for step in range(GROUP):
                slope = slope_ref[0, start + first + step].astype(F32)
                d_pre = d_edges[:, edge_width * step : edge_width * (step + 1)] * slope
                right_sum = right_sum + d_pre
                lefts.append(jnp.sum(d_pre, axis=0, keepdims=True))
        right_s[...] = right_sum
        left_s[pl.ds(start, CHUNK), :] = jnp.concatenate(lefts, axis=0)
        return carry

    lax.fori_loop(0, block // CHUNK, step_group, 0)
    nodes = nodes_ref[...]
    sender = sender_ref[0]
    query_wide = spread(dot(nodes, wq_ref[...]).astype(BF16), heads)
    datt_wide = spread(dot(dout_ref[...], wo_ref[...], 1, 1).astype(BF16), heads)
    keys = dot(sender, wk_ref[...]).astype(BF16)
    dlogit = dlogit_s[...]
    grad_query = gather_heads(dot(dlogit, keys), heads) * scale
    grad_keys = dot(dlogit, query_wide, 0, 0) * scale
    grad_values = dot(probs_s[...], datt_wide, 0, 0)
    node_ref[local] += dot(grad_query.astype(BF16), wq_ref[...], 1, 1) + 0.5 * dot(
        left_s[...].astype(BF16), wl_ref[...], 1, 1
    )
    send_grad = (
        dot(grad_keys.astype(BF16), wk_ref[...], 1, 1)
        + dot(grad_values.astype(BF16), wv_ref[...], 1, 1)
        + 0.5 * dot(right_s[...].astype(BF16), wr_ref[...], 1, 1)
    )

    @pl.when(place < own_blocks)
    def _():
        node_ref[place] += send_grad

    @pl.when(place >= own_blocks)
    def _():
        leaving_ref[place - own_blocks] = send_grad.astype(BF16)

    grad_ev_ref[...] += dot(ctx_s[...], datt_wide, 0, 0)


MESH = pl.DeviceIdType.MESH


def peers_of(axis, count):
    me = lax.axis_index(axis)
    return me, [
        (offset, lax.rem(me + offset, count), lax.rem(me + count - offset, count))
        for offset in range(1, count)
    ]


def meet(groups):
    barrier = pltpu.get_barrier_semaphore()
    total = 0
    for axis, peers in groups:
        for _, target, _ in peers:
            pl.semaphore_signal(barrier, inc=1, device_id={axis: target}, device_id_type=MESH)
            total += 1
    pl.semaphore_wait(barrier, total)


def post(axis, peers, sems, source, landing):
    copies = []
    for offset, target, _ in peers:
        copy = pltpu.make_async_remote_copy(
            src_ref=source(target),
            dst_ref=landing,
            send_sem=sems.at[0, offset],
            recv_sem=sems.at[1, offset],
            device_id={axis: target},
            device_id_type=MESH,
        )
        copy.start()
        copies.append(copy)
    return copies


def fetch_kernel(
    n_recv, pairs_ref, nodes_ref, table_ref, asked_ref, want_s, ask_s, reply_s, got_s, ask_sems, reply_sems
):
    me, peers = peers_of("recv", n_recv)
    blocks = nodes_ref.shape[0]
    for _, target, _ in peers:
        wanted = 0
        for slot in range(pairs_ref.shape[1]):
            sender = pairs_ref[1, slot]
            wanted = wanted + jnp.where(sender // blocks == target, sender % blocks, 0)
        want_s[target] = jnp.full(want_s.shape[1:], wanted, jnp.int32).astype(F32)
    meet([("recv", peers)])
    asks = post("recv", peers, ask_sems, lambda target: want_s.at[target], ask_s.at[me])
    nodes = nodes_ref[...].astype(F32)
    for copy in asks:
        copy.wait_recv()
    replies = []
    for peer in peers:
        offset, target, _ = peer
        ask = ask_s[target][0:1, 0:1]
        reply = nodes[0]
        for at in range(1, nodes.shape[0]):
            reply = jnp.where(ask == float(at), nodes[at], reply)
        reply_s[offset] = reply.astype(BF16)
        replies += post("recv", [peer], reply_sems, lambda target: reply_s.at[offset], got_s.at[me])
    asked_ref[...] = jnp.zeros_like(asked_ref)
    table_ref[:blocks] = nodes_ref[...]
    table_ref[blocks + me] = jnp.zeros_like(nodes_ref[0])
    for _, target, _ in peers:
        asked_ref[target] = ask_s[target]
    for copy, (_, _, source) in zip(replies, peers):
        copy.wait_recv()
        table_ref[blocks + source] = got_s[source]
    for copy in asks + replies:
        copy.wait_send()


def join_kernel(n_send, stats_ref, joined_ref, all_s, sems):
    me, peers = peers_of("send", n_send)
    meet([("send", peers)])
    copies = post("send", peers, sems, lambda target: stats_ref, all_s.at[me])
    slots = stats_ref.shape[0]
    all_s[me] = stats_ref[...]
    for copy in copies:
        copy.wait_recv()
    for slot in range(slots):
        lands = stats_ref[slot, 3]
        top = stats_ref[slot, 0]
        for device in range(n_send):
            for other in range(slots):
                top = jnp.maximum(
                    top,
                    jnp.where(all_s[device, other, 3] == lands, all_s[device, other, 0], NEG_LARGE),
                )
        total = jnp.zeros_like(top)
        delta = jnp.zeros_like(top)
        for device in range(n_send):
            for other in range(slots):
                part = jnp.where(
                    all_s[device, other, 3] == lands, jnp.exp(all_s[device, other, 0] - top), 0.0
                )
                total = total + part * all_s[device, other, 1]
                delta = delta + part * all_s[device, other, 2]
        joined_ref[slot, 0] = top + jnp.log(total)
        joined_ref[slot, 1] = delta / total
    for copy in copies:
        copy.wait_send()


def tail_kernel(
    n_recv,
    n_send,
    att_ref,
    node_ref,
    leaving_ref,
    asked_ref,
    ev_ref,
    bias_ref,
    nodes_ref,
    dout_ref,
    wo_ref,
    mixed_ref,
    grad_ref,
    bias_out_ref,
    ev_out_ref,
    back_s,
    out_a,
    in_a,
    mix_s,
    small_s,
    small_all,
    acc_s,
    out_n,
    in_n,
    fin_s,
    back_sems,
    a_sems,
    mix_sems,
    small_sems,
    small_all_sems,
    n_sems,
    fin_sems,
):
    row, row_peers = peers_of("recv", n_recv)
    col, col_peers = peers_of("send", n_send)
    blocks, block, width = node_ref.shape
    rows = blocks * block
    share = rows // n_send
    ev_share = ev_ref.shape[0] // n_send
    heads, edge_width = bias_ref.shape
    sums = att_ref[...].reshape(rows, width)
    meet([("recv", row_peers), ("send", col_peers)])
    backs = post("recv", row_peers, back_sems, lambda target: leaving_ref.at[target], back_s.at[row])
    for part in range(n_send):
        out_a[part, :share] = sums[part * share : (part + 1) * share].astype(BF16)
        out_a[part, share : share + ev_share] = ev_ref[
            part * ev_share : (part + 1) * ev_share
        ].astype(BF16)
        out_a[part, share + ev_share :] = jnp.zeros((BIAS_ROWS, width), BF16)
    bias = jnp.concatenate([bias_ref[...], jnp.zeros_like(bias_ref)], axis=0).astype(BF16)
    out_a[0, share + ev_share :, :edge_width] = bias
    sent_a = post("send", col_peers, a_sems, lambda target: out_a.at[target], in_a.at[col])
    acc_s[...] = node_ref[...].reshape(rows, width)
    total = out_a[col].astype(F32)
    for copy, (_, _, source) in zip(sent_a, col_peers):
        copy.wait_recv()
        total = total + in_a[source].astype(F32)
    small_s[row] = total[share:].astype(BF16)
    smalls = post("recv", row_peers, small_sems, lambda target: small_s.at[row], small_s.at[row])
    here = pl.ds(pl.multiple_of(col * share, share), share)
    mixed = nodes_ref[here, :].astype(F32) + dot(total[:share].astype(BF16), wo_ref[...])
    mix_s[col] = mixed.astype(BF16)
    mixes = post("send", col_peers, mix_sems, lambda target: mix_s.at[col], mix_s.at[col])
    for copy, (_, _, source) in zip(backs, row_peers):
        copy.wait_recv()
        asked = asked_ref[source][0:1, 0:1]
        landed = back_s[source].astype(F32)
        for at in range(blocks):
            acc_s[at * block : (at + 1) * block, :] += jnp.where(asked == float(at), landed, 0.0)
    for part in range(n_send):
        out_n[part] = acc_s[part * share : (part + 1) * share, :].astype(BF16)
    sent_n = post("send", col_peers, n_sems, lambda target: out_n.at[target], in_n.at[col])
    for copy in smalls:
        copy.wait_recv()
    small = small_s[0].astype(F32)
    for at in range(1, n_recv):
        small = small + small_s[at].astype(F32)
    small_all[col] = small.astype(BF16)
    small_alls = post(
        "send", col_peers, small_all_sems, lambda target: small_all.at[col], small_all.at[col]
    )
    total = out_n[col].astype(F32)
    for copy, (_, _, source) in zip(sent_n, col_peers):
        copy.wait_recv()
        total = total + in_n[source].astype(F32)
    fin_s[col] = total.astype(BF16)
    fins = post("send", col_peers, fin_sems, lambda target: fin_s.at[col], fin_s.at[col])
    for copy in mixes:
        copy.wait_recv()
    mixed_ref[...] = mix_s[...].reshape(rows, width)
    for copy in small_alls:
        copy.wait_recv()
    for part in range(n_send):
        ev_out_ref[part * ev_share : (part + 1) * ev_share, :] = small_all[part, :ev_share].astype(F32)
    bias_out_ref[...] = small_all[0, ev_share:, :edge_width].astype(F32)[:heads]
    for copy in fins:
        copy.wait_recv()
    for part in range(n_send):
        span = slice(part * share, (part + 1) * share)
        grad_ref[span, :] = dout_ref[span, :].astype(F32) + fin_s[part].astype(F32)
    for copy in backs + sent_a + smalls + mixes + sent_n + small_alls + fins:
        copy.wait_send()


def table_place(own_blocks, slot, pairs):
    owner = pairs[1, slot] // own_blocks
    return jnp.where(
        owner == pairs[0, slot] // own_blocks, pairs[1, slot] % own_blocks, own_blocks + owner
    )


def whole_spec(array):
    zeros = (0,) * array.ndim
    return pl.BlockSpec(array.shape, lambda slot, *_: zeros)


def slot_spec(shape):
    rest = (0,) * (len(shape) - 1)
    return pl.BlockSpec((1,) + tuple(shape[1:]), lambda slot, *_: (slot,) + rest)


def body(
    nodes,
    frames,
    pairs,
    masks,
    d_out,
    w_query,
    w_key,
    w_value,
    w_left,
    w_right,
    frame_edge,
    w_bias,
    w_edge_value,
    w_out,
):
    rows, width = nodes.shape
    slots, block = masks.shape
    nb_local = rows // block
    heads, edge_width = w_bias.shape
    att_width = w_query.shape[1]
    scale = (att_width // heads) ** (-0.5)
    n_recv = lax.axis_size("recv")
    n_send = lax.axis_size("send")

    node_blocks = nodes.reshape(nb_local, block, width)
    in_vmem = pl.BlockSpec(memory_space=pltpu.VMEM)
    asks_shape = (n_recv, 8, 128)
    table, asked = pl.pallas_call(
        functools.partial(fetch_kernel, n_recv),
        in_specs=[pl.BlockSpec(memory_space=pltpu.SMEM), in_vmem],
        out_specs=[in_vmem] * 2,
        out_shape=[
            jax.ShapeDtypeStruct((nb_local + n_recv, block, width), BF16),
            jax.ShapeDtypeStruct(asks_shape, F32),
        ],
        scratch_shapes=[
            pltpu.VMEM(asks_shape, F32),
            pltpu.VMEM(asks_shape, F32),
            pltpu.VMEM((n_recv, block, width), BF16),
            pltpu.VMEM((n_recv, block, width), BF16),
            pltpu.SemaphoreType.DMA((2, n_recv)),
            pltpu.SemaphoreType.DMA((2, n_recv)),
        ],
        compiler_params=pltpu.CompilerParams(
            collective_id=1, has_side_effects=True, vmem_limit_bytes=VMEM_LIMIT
        ),
        name="fetch",
    )(pairs, node_blocks)

    frame_rows = frames.reshape(-1, 1, block)
    mask_rows = masks.reshape(slots, 1, block)
    edge_row = frame_edge.reshape(1, edge_width)
    recv_spec = pl.BlockSpec((block, width), lambda slot, pairs, *_: (pairs[0, slot] % nb_local, 0))
    sender_spec = pl.BlockSpec(
        (1, block, width), lambda slot, pairs, *_: (table_place(nb_local, slot, pairs), 0, 0)
    )
    logit_shape = (slots, block, heads, block)
    sums_shape = (slots, block, 2 * heads, edge_width)
    slope_shape = (slots, block, block, edge_width)
    att_shape = (slots, block, att_width)
    stats_shape = (slots, 4, block * heads // 128, 128)
    weights = (w_query, w_key, w_value, w_left, w_right, edge_row, w_bias, w_edge_value, w_out)
    forward = pl.pallas_call(
        functools.partial(forward_kernel, scale, nb_local),
        grid_spec=pltpu.PrefetchScalarGridSpec(
            num_scalar_prefetch=2,
            grid=(slots,),
            in_specs=[
                pl.BlockSpec((1, 1, block), lambda slot, pairs, *_: (pairs[1, slot], 0, 0)),
                slot_spec(mask_rows.shape),
                recv_spec,
                recv_spec,
                sender_spec,
            ]
            + [whole_spec(weight) for weight in weights],
            out_specs=[
                slot_spec(shape)
                for shape in (
                    logit_shape, logit_shape, slope_shape, sums_shape, sums_shape, att_shape, stats_shape,
                )
            ],
            scratch_shapes=[
                pltpu.VMEM((block, edge_width), F32),
                pltpu.VMEM((block, block, edge_width), BF16),
                pltpu.VMEM((block * heads, block), BF16),
            ],
        ),
        out_shape=[
            jax.ShapeDtypeStruct(logit_shape, F32),
            jax.ShapeDtypeStruct(logit_shape, F32),
            jax.ShapeDtypeStruct(slope_shape, BF16),
            jax.ShapeDtypeStruct(sums_shape, BF16),
            jax.ShapeDtypeStruct(sums_shape, BF16),
            jax.ShapeDtypeStruct(att_shape, F32),
            jax.ShapeDtypeStruct(stats_shape, F32),
        ],
        compiler_params=pltpu.CompilerParams(vmem_limit_bytes=VMEM_LIMIT),
        name="forward",
    )
    logits, dprobs, slopes, sums, wides, att_parts, stats = forward(
        pairs, frames,
        frame_rows, mask_rows, nodes, d_out, table, *weights,
    )

    joined_shape = (slots, 2) + stats.shape[2:]
    joined = pl.pallas_call(
        functools.partial(join_kernel, n_send),
        in_specs=[in_vmem],
        out_specs=in_vmem,
        out_shape=jax.ShapeDtypeStruct(joined_shape, F32),
        scratch_shapes=[
            pltpu.VMEM((n_send,) + stats.shape, F32),
            pltpu.SemaphoreType.DMA((2, n_send)),
        ],
        compiler_params=pltpu.CompilerParams(
            collective_id=2, has_side_effects=True, vmem_limit_bytes=VMEM_LIMIT
        ),
        name="join",
    )(stats)

    weights = (w_query, w_key, w_value, w_left, w_right, w_out)
    node_shape = (nb_local, block, width)
    away_shape = (n_recv, block, width)
    att_sum_shape = (nb_local, block, att_width)
    backward = pl.pallas_call(
        functools.partial(backward_kernel, scale, nb_local),
        grid_spec=pltpu.PrefetchScalarGridSpec(
            num_scalar_prefetch=1,
            grid=(slots,),
            in_specs=[slot_spec(mask_rows.shape), recv_spec, recv_spec, sender_spec]
            + [whole_spec(weight) for weight in weights]
            + [
                slot_spec(shape)
                for shape in (
                    logit_shape, logit_shape, slope_shape, sums_shape, sums_shape, att_shape, stats_shape,
                    joined.shape,
                )
            ],
            out_specs=[
                whole_spec(node_blocks),
                whole_spec(jax.ShapeDtypeStruct(away_shape, BF16)),
                whole_spec(jax.ShapeDtypeStruct(att_sum_shape, F32)),
                whole_spec(w_edge_value),
                whole_spec(w_bias),
            ],
            scratch_shapes=[
                pltpu.VMEM((block * heads, block), BF16),
                pltpu.VMEM((block * heads, block), BF16),
                pltpu.VMEM((block * heads, edge_width), BF16),
                pltpu.VMEM((block, edge_width), F32),
                pltpu.VMEM((block, edge_width), F32),
                pltpu.VMEM((CHUNK // GROUP, GROUP * 2 * heads, GROUP * edge_width), BF16),
            ],
        ),
        out_shape=[
            jax.ShapeDtypeStruct(node_shape, F32),
            jax.ShapeDtypeStruct(away_shape, BF16),
            jax.ShapeDtypeStruct(att_sum_shape, F32),
            jax.ShapeDtypeStruct(w_edge_value.shape, F32),
            jax.ShapeDtypeStruct(w_bias.shape, F32),
        ],
        compiler_params=pltpu.CompilerParams(vmem_limit_bytes=VMEM_LIMIT),
        name="backward",
    )
    node_sum, leaving, att, grad_ev, grad_bias = backward(
        pairs, mask_rows, nodes, d_out, table, *weights,
        logits, dprobs, slopes, sums, wides, att_parts, stats, joined,
    )

    share = rows // n_send
    ev_share = edge_width // n_send
    tail_rows = ev_share + BIAS_ROWS
    return pl.pallas_call(
        functools.partial(tail_kernel, n_recv, n_send),
        in_specs=[in_vmem] * 9,
        out_specs=[in_vmem] * 4,
        out_shape=[
            jax.ShapeDtypeStruct((rows, width), BF16),
            jax.ShapeDtypeStruct((rows, width), F32),
            jax.ShapeDtypeStruct((heads, edge_width), F32),
            jax.ShapeDtypeStruct((edge_width, att_width), F32),
        ],
        scratch_shapes=[
            pltpu.VMEM(away_shape, BF16),
            pltpu.VMEM((n_send, share + tail_rows, att_width), BF16),
            pltpu.VMEM((n_send, share + tail_rows, att_width), BF16),
            pltpu.VMEM((n_send, share, width), BF16),
            pltpu.VMEM((n_recv, tail_rows, att_width), BF16),
            pltpu.VMEM((n_send, tail_rows, att_width), BF16),
            pltpu.VMEM((rows, width), F32),
            pltpu.VMEM((n_send, share, width), BF16),
            pltpu.VMEM((n_send, share, width), BF16),
            pltpu.VMEM((n_send, share, width), BF16),
            pltpu.SemaphoreType.DMA((2, n_recv)),
            pltpu.SemaphoreType.DMA((2, n_send)),
            pltpu.SemaphoreType.DMA((2, n_send)),
            pltpu.SemaphoreType.DMA((2, n_recv)),
            pltpu.SemaphoreType.DMA((2, n_send)),
            pltpu.SemaphoreType.DMA((2, n_send)),
            pltpu.SemaphoreType.DMA((2, n_send)),
        ],
        compiler_params=pltpu.CompilerParams(
            collective_id=3, has_side_effects=True, vmem_limit_bytes=TAIL_LIMIT
        ),
        name="tail",
    )(att, node_sum, leaving, asked, grad_ev, grad_bias, nodes, d_out, w_out)


def solution(mesh):
    in_specs = (
        P("recv", None),
        P(),
        P(None, ("recv", "send")),
        P(("recv", "send"), None),
        P("recv", None),
        P(),
        P(),
        P(),
        P(),
        P(),
        P(),
        P(),
        P(),
        P(),
    )
    out_specs = (P("recv", None), P("recv", None), P(), P())
    return jax.shard_map(body, mesh=mesh, in_specs=in_specs, out_specs=out_specs, check_vma=False)
```

```python
import functools

import jax
import jax.numpy as jnp
from jax import lax
from jax.experimental import pallas as pl
from jax.experimental.pallas import tpu as pltpu
from jax.sharding import PartitionSpec as P

NEG_LARGE = -1e30
CHUNK = 16
WIDE_CHUNK = 32
GROUP = 8
BIAS_ROWS = 16
VMEM_LIMIT = 60 * 2**20
TAIL_LIMIT = 60 * 2**20
F32 = jnp.float32
BF16 = jnp.bfloat16


def dot(first, second, first_dim=1, second_dim=0):
    return lax.dot_general(
        first, second, (((first_dim,), (second_dim,)), ((), ())), preferred_element_type=F32
    )


def to_column(row):
    count = row.shape[1]
    eye = lax.broadcasted_iota(jnp.int32, (count, count), 0) == lax.broadcasted_iota(
        jnp.int32, (count, count), 1
    )
    return jnp.sum(jnp.where(eye, row, 0.0), axis=1, keepdims=True)


def to_row(column):
    count = column.shape[0]
    eye = lax.broadcasted_iota(jnp.int32, (count, count), 0) == lax.broadcasted_iota(
        jnp.int32, (count, count), 1
    )
    return jnp.sum(jnp.where(eye, column, 0.0), axis=0, keepdims=True)


def head_mask(heads, width):
    return lax.broadcasted_iota(jnp.int32, (heads, width), 1) // (
        width // heads
    ) == lax.broadcasted_iota(jnp.int32, (heads, width), 0)


def owner_matrix(count, heads, rows_first):
    shape = (count * heads, count) if rows_first else (count, count * heads)
    wide = lax.broadcasted_iota(jnp.int32, shape, 0 if rows_first else 1) // heads
    narrow = lax.broadcasted_iota(jnp.int32, shape, 1 if rows_first else 0)
    return jnp.where(wide == narrow, 1.0, 0.0).astype(BF16)


def spread(rows, heads):
    count, width = rows.shape
    mask = head_mask(heads, width)
    wide = dot(owner_matrix(count, heads, True), rows).reshape(count, heads, width)
    return jnp.where(mask[None], wide, 0.0).reshape(count * heads, width).astype(BF16)


def gather_heads(wide, heads):
    count, width = wide.shape
    mask = head_mask(heads, width)
    kept = jnp.where(mask[None], wide.reshape(count // heads, heads, width), 0.0)
    return dot(owner_matrix(count // heads, heads, False), kept.reshape(count, width).astype(BF16))


def forward_kernel(
    scale,
    own_blocks,
    pairs_ref,
    frames_ref,
    frame_row_ref,
    mask_ref,
    nodes_ref,
    dout_ref,
    sender_ref,
    wq_ref,
    wk_ref,
    wv_ref,
    wl_ref,
    wr_ref,
    fe_ref,
    wb_ref,
    wev_ref,
    wo_ref,
    logit_ref,
    dprob_ref,
    slope_ref,
    sums_ref,
    wide_ref,
    att_ref,
    stats_ref,
    left_s,
    edge_s,
    probs_s,
    scores_s,
    dvalues_s,
):
    slot = pl.program_id(0)
    heads, edge_width = wb_ref.shape
    block = nodes_ref.shape[0]
    nodes = nodes_ref[...]
    sender = sender_ref[0]
    query = dot(nodes, wq_ref[...]).astype(BF16)
    left_s[...] = dot(nodes, wl_ref[...]) * 0.5
    datt = dot(dout_ref[...], wo_ref[...], 1, 1).astype(BF16)
    keys = dot(sender, wk_ref[...]).astype(BF16)
    values = dot(sender, wv_ref[...]).astype(BF16)
    right = dot(sender, wr_ref[...]) * 0.5
    right_same = (right + fe_ref[...].astype(F32) * 0.5).astype(BF16)
    right = right.astype(BF16)
    frame_col = jnp.broadcast_to(
        to_column(frame_row_ref[0].astype(F32)), (block, edge_width)
    ).astype(BF16)
    datt_wide = spread(datt, heads)
    scores_s[...] = (dot(spread(query, heads), keys, 1, 1) * scale).reshape(block, heads, block)
    dvalues_s[...] = dot(datt_wide, values, 1, 1).reshape(block, heads, block)
    dctx = dot(datt_wide, wev_ref[...], 1, 1).reshape(block, heads, edge_width)
    bias = jnp.broadcast_to(wb_ref[...].astype(F32)[None], dctx.shape)
    wide_ref[0] = jnp.concatenate([bias, dctx], axis=1).astype(BF16)
    recv_start = pairs_ref[0, slot] * block

    one = jnp.ones((), BF16)

    def edge_step(group, carry):
        start = group * WIDE_CHUNK
        left_rows = left_s[pl.ds(start, WIDE_CHUNK), :].astype(BF16)
        for step in range(0, WIDE_CHUNK, 2):
            edges = []
            for at in (step, step + 1):
                frame = frames_ref[recv_start + start + at].astype(F32).astype(BF16)
                half = left_rows[at : at + 1] + jnp.where(frame_col == frame, right_same, right)
                turn = jnp.tanh(half)
                gain = half * turn
                edge = half + gain
                slope_ref[0, start + at] = (one + turn) * (one + (half - gain))
                edge_s[start + at] = edge
                edges.append(edge)
            wide = wide_ref[0, pl.ds(start + step, 2)].reshape(4 * heads, edge_width)
            both = dot(wide, jnp.concatenate(edges, axis=0), 1, 1)
            for at in (0, 1):
                part = both[2 * heads * at : 2 * heads * (at + 1), block * at : block * (at + 1)]
                here = start + step + at
                logit_ref[0, here] = scores_s[here] + part[:heads]
                dprob_ref[0, here] = dvalues_s[here] + part[heads:]
        return carry

    lax.fori_loop(0, block // WIDE_CHUNK, edge_step, 0)
    valid = mask_ref[0] > 0

    def soft_step(step_at, carry):
        for sub in range(WIDE_CHUNK // CHUNK):
            group = step_at * (WIDE_CHUNK // CHUNK) + sub
            start = group * CHUNK
            rows = pl.ds(start * heads, CHUNK * heads)
            logits = logit_ref[0, pl.ds(start, CHUNK)].reshape(CHUNK * heads, block)
            dprob = dprob_ref[0, pl.ds(start, CHUNK)].reshape(CHUNK * heads, block)
            logits = jnp.where(valid, logits, NEG_LARGE)
            top = jnp.max(logits, axis=1, keepdims=True)
            probs = jnp.where(valid, jnp.exp(logits - top), 0.0)
            weighted = probs * dprob
            stats_ref[0, 0, pl.ds(group, 1), :] = to_row(top)
            stats_ref[0, 1, pl.ds(group, 1), :] = to_row(jnp.sum(probs, axis=1, keepdims=True))
            stats_ref[0, 2, pl.ds(group, 1), :] = to_row(jnp.sum(weighted, axis=1, keepdims=True))
            probs_s[rows, :] = probs.astype(BF16)
            pair = jnp.concatenate(
                [probs.reshape(CHUNK, heads, block), weighted.reshape(CHUNK, heads, block)], axis=1
            ).astype(BF16)
            for step in range(0, CHUNK, 2):
                edges = jnp.concatenate([edge_s[start + step], edge_s[start + step + 1]], axis=1)
                both = dot(pair[step : step + 2].reshape(4 * heads, block), edges).astype(BF16)
                sums_ref[0, start + step] = both[: 2 * heads, :edge_width]
                sums_ref[0, start + step + 1] = both[2 * heads :, edge_width:]
        return carry

    lax.fori_loop(0, block // WIDE_CHUNK, soft_step, 0)
    stats_ref[0, 3] = jnp.full(stats_ref.shape[2:], pairs_ref[0, slot].astype(F32), F32)
    ctx = sums_ref[0].astype(F32)[:, :heads].reshape(block * heads, edge_width).astype(BF16)
    att_ref[0] = gather_heads(dot(probs_s[...], values) + dot(ctx, wev_ref[...]), heads)


def backward_kernel(
    scale,
    own_blocks,
    pairs_ref,
    mask_ref,
    nodes_ref,
    dout_ref,
    sender_ref,
    wq_ref,
    wk_ref,
    wv_ref,
    wl_ref,
    wr_ref,
    wo_ref,
    logit_ref,
    dprob_ref,
    slope_ref,
    sums_ref,
    wide_ref,
    att_in_ref,
    stats_ref,
    joined_ref,
    node_ref,
    leaving_ref,
    att_ref,
    grad_ev_ref,
    grad_bias_ref,
    probs_s,
    dlogit_s,
    ctx_s,
    left_s,
    right_s,
    diagonal_s,
):
    slot = pl.program_id(0)
    heads = logit_ref.shape[2]
    block = nodes_ref.shape[0]
    edge_width = wide_ref.shape[3]
    width = wq_ref.shape[1]
    mask = head_mask(heads, width)
    valid = mask_ref[0] > 0

    @pl.when(slot == 0)
    def _():
        grad_ev_ref[...] = jnp.zeros_like(grad_ev_ref)
        grad_bias_ref[...] = jnp.zeros_like(grad_bias_ref)
        node_ref[...] = jnp.zeros_like(node_ref)
        diagonal_s[...] = jnp.zeros_like(diagonal_s)
        leaving_ref[...] = jnp.zeros_like(leaving_ref)
        att_ref[...] = jnp.zeros_like(att_ref)

    local = pairs_ref[0, slot] % own_blocks
    place = table_place(own_blocks, slot, pairs_ref)
    right_s[...] = jnp.zeros_like(right_s)

    def step_group(step_at, carry):
        for sub in range(WIDE_CHUNK // CHUNK):
            group = step_at * (WIDE_CHUNK // CHUNK) + sub
            start = group * CHUNK
            rows = pl.ds(start * heads, CHUNK * heads)
            lse = joined_ref[0, 0, pl.ds(group, 1), :]
            lse_col = to_column(lse)
            delta_col = to_column(joined_ref[0, 1, pl.ds(group, 1), :])
            factor_col = to_column(jnp.exp(stats_ref[0, 0, pl.ds(group, 1), :] - lse))
            logits = logit_ref[0, pl.ds(start, CHUNK)].reshape(CHUNK * heads, block)
            dprob = dprob_ref[0, pl.ds(start, CHUNK)].reshape(CHUNK * heads, block)
            probs = jnp.where(valid, jnp.exp(logits - lse_col), 0.0)
            dlogit = probs * (dprob - delta_col)
            probs_s[rows, :] = probs.astype(BF16)
            dlogit_s[rows, :] = dlogit.astype(BF16)
            sums = sums_ref[0, pl.ds(start, CHUNK)].astype(F32)
            ctx = sums[:, :heads].reshape(CHUNK * heads, edge_width) * factor_col
            ctx_s[rows, :] = ctx.astype(BF16)
            moved = sums[:, heads:].reshape(CHUNK * heads, edge_width) * factor_col - ctx * delta_col
            grad_bias_ref[...] += jnp.sum(moved.reshape(CHUNK, heads, edge_width), axis=0)
            factor = jnp.sum(
                jnp.where(mask[None], factor_col.reshape(CHUNK, heads, 1), 0.0), axis=1
            )
            att_ref[local, pl.ds(start, CHUNK), :] += att_in_ref[0, pl.ds(start, CHUNK), :] * factor
            pair = jnp.concatenate(
                [dlogit.reshape(CHUNK, heads, block), probs.reshape(CHUNK, heads, block)], axis=1
            ).astype(BF16)
            right_sum = right_s[...]
            lefts = []
            for half in range(CHUNK // GROUP):
                first = half * GROUP
                for step in range(GROUP):
                    diagonal_s[
                        sub * (CHUNK // GROUP) + half,
                        2 * heads * step : 2 * heads * (step + 1),
                        edge_width * step : edge_width * (step + 1),
                    ] = wide_ref[0, start + first + step]
                pairs = pair[first : first + GROUP].reshape(GROUP * 2 * heads, block)
                d_edges = dot(pairs, diagonal_s[sub * (CHUNK // GROUP) + half], 0, 0)
                for step in range(GROUP):
                    slope = slope_ref[0, start + first + step].astype(F32)
                    d_pre = d_edges[:, edge_width * step : edge_width * (step + 1)] * slope
                    right_sum = right_sum + d_pre
                    lefts.append(jnp.sum(d_pre, axis=0, keepdims=True))
            right_s[...] = right_sum
            left_s[pl.ds(start, CHUNK), :] = jnp.concatenate(lefts, axis=0)
        return carry

    lax.fori_loop(0, block // WIDE_CHUNK, step_group, 0)
    nodes = nodes_ref[...]
    sender = sender_ref[0]
    query_wide = spread(dot(nodes, wq_ref[...]).astype(BF16), heads)
    datt_wide = spread(dot(dout_ref[...], wo_ref[...], 1, 1).astype(BF16), heads)
    keys = dot(sender, wk_ref[...]).astype(BF16)
    dlogit = dlogit_s[...]
    grad_query = gather_heads(dot(dlogit, keys), heads) * scale
    grad_keys = dot(dlogit, query_wide, 0, 0) * scale
    grad_values = dot(probs_s[...], datt_wide, 0, 0)
    node_ref[local] += dot(grad_query.astype(BF16), wq_ref[...], 1, 1) + 0.5 * dot(
        left_s[...].astype(BF16), wl_ref[...], 1, 1
    )
    send_grad = (
        dot(grad_keys.astype(BF16), wk_ref[...], 1, 1)
        + dot(grad_values.astype(BF16), wv_ref[...], 1, 1)
        + 0.5 * dot(right_s[...].astype(BF16), wr_ref[...], 1, 1)
    )

    @pl.when(place < own_blocks)
    def _():
        node_ref[place] += send_grad

    @pl.when(place >= own_blocks)
    def _():
        leaving_ref[place - own_blocks] = send_grad.astype(BF16)

    grad_ev_ref[...] += dot(ctx_s[...], datt_wide, 0, 0)


MESH = pl.DeviceIdType.MESH


def peers_of(axis, count):
    me = lax.axis_index(axis)
    return me, [
        (offset, lax.rem(me + offset, count), lax.rem(me + count - offset, count))
        for offset in range(1, count)
    ]


def meet(groups):
    barrier = pltpu.get_barrier_semaphore()
    total = 0
    for axis, peers in groups:
        for _, target, _ in peers:
            pl.semaphore_signal(barrier, inc=1, device_id={axis: target}, device_id_type=MESH)
            total += 1
    pl.semaphore_wait(barrier, total)


def post(axis, peers, sems, source, landing):
    copies = []
    for offset, target, _ in peers:
        copy = pltpu.make_async_remote_copy(
            src_ref=source(target),
            dst_ref=landing,
            send_sem=sems.at[0, offset],
            recv_sem=sems.at[1, offset],
            device_id={axis: target},
            device_id_type=MESH,
        )
        copy.start()
        copies.append(copy)
    return copies


def fetch_kernel(
    n_recv, pairs_ref, nodes_ref, table_ref, asked_ref, want_s, ask_s, reply_s, got_s, ask_sems, reply_sems
):
    me, peers = peers_of("recv", n_recv)
    blocks = nodes_ref.shape[0]
    for _, target, _ in peers:
        wanted = 0
        for slot in range(pairs_ref.shape[1]):
            sender = pairs_ref[1, slot]
            wanted = wanted + jnp.where(sender // blocks == target, sender % blocks, 0)
        want_s[target] = jnp.full(want_s.shape[1:], wanted, jnp.int32).astype(F32)
    meet([("recv", peers)])
    asks = post("recv", peers, ask_sems, lambda target: want_s.at[target], ask_s.at[me])
    nodes = nodes_ref[...].astype(F32)
    for copy in asks:
        copy.wait_recv()
    replies = []
    for peer in peers:
        offset, target, _ = peer
        ask = ask_s[target][0:1, 0:1]
        reply = nodes[0]
        for at in range(1, nodes.shape[0]):
            reply = jnp.where(ask == float(at), nodes[at], reply)
        reply_s[offset] = reply.astype(BF16)
        replies += post("recv", [peer], reply_sems, lambda target: reply_s.at[offset], got_s.at[me])
    asked_ref[...] = jnp.zeros_like(asked_ref)
    table_ref[:blocks] = nodes_ref[...]
    table_ref[blocks + me] = jnp.zeros_like(nodes_ref[0])
    for _, target, _ in peers:
        asked_ref[target] = ask_s[target]
    for copy, (_, _, source) in zip(replies, peers):
        copy.wait_recv()
        table_ref[blocks + source] = got_s[source]
    for copy in asks + replies:
        copy.wait_send()


def join_kernel(n_send, stats_ref, joined_ref, all_s, sems):
    me, peers = peers_of("send", n_send)
    meet([("send", peers)])
    copies = post("send", peers, sems, lambda target: stats_ref, all_s.at[me])
    slots = stats_ref.shape[0]
    all_s[me] = stats_ref[...]
    for copy in copies:
        copy.wait_recv()
    for slot in range(slots):
        lands = stats_ref[slot, 3]
        top = stats_ref[slot, 0]
        for device in range(n_send):
            for other in range(slots):
                top = jnp.maximum(
                    top,
                    jnp.where(all_s[device, other, 3] == lands, all_s[device, other, 0], NEG_LARGE),
                )
        total = jnp.zeros_like(top)
        delta = jnp.zeros_like(top)
        for device in range(n_send):
            for other in range(slots):
                part = jnp.where(
                    all_s[device, other, 3] == lands, jnp.exp(all_s[device, other, 0] - top), 0.0
                )
                total = total + part * all_s[device, other, 1]
                delta = delta + part * all_s[device, other, 2]
        joined_ref[slot, 0] = top + jnp.log(total)
        joined_ref[slot, 1] = delta / total
    for copy in copies:
        copy.wait_send()


def tail_kernel(
    n_recv,
    n_send,
    att_hbm,
    node_hbm,
    leaving_ref,
    asked_ref,
    ev_hbm,
    bias_ref,
    nodes_ref,
    dout_ref,
    wo_ref,
    mixed_ref,
    grad_ref,
    bias_out_ref,
    ev_out_ref,
    att_ref,
    node_ref,
    ev_ref,
    load_sems,
    back_s,
    out_a,
    in_a,
    mix_s,
    small_s,
    small_all,
    acc_s,
    out_n,
    in_n,
    fin_s,
    back_sems,
    a_sems,
    mix_sems,
    small_sems,
    small_all_sems,
    n_sems,
    fin_sems,
):
    row, row_peers = peers_of("recv", n_recv)
    col, col_peers = peers_of("send", n_send)
    blocks, block, width = node_ref.shape
    rows = blocks * block
    share = rows // n_send
    ev_share = ev_ref.shape[0] // n_send
    heads, edge_width = bias_ref.shape
    loads = [
        pltpu.make_async_copy(source, target, load_sems.at[at])
        for at, (source, target) in enumerate(
            ((att_hbm, att_ref), (ev_hbm, ev_ref), (node_hbm, node_ref))
        )
    ]
    for load in loads:
        load.start()
    meet([("recv", row_peers), ("send", col_peers)])
    backs = post("recv", row_peers, back_sems, lambda target: leaving_ref.at[target], back_s.at[row])
    loads[0].wait()
    loads[1].wait()
    sums = att_ref[...].reshape(rows, width)
    for part in range(n_send):
        out_a[part, :share] = sums[part * share : (part + 1) * share].astype(BF16)
        out_a[part, share : share + ev_share] = ev_ref[
            part * ev_share : (part + 1) * ev_share
        ].astype(BF16)
        out_a[part, share + ev_share :] = jnp.zeros((BIAS_ROWS, width), BF16)
    bias = jnp.concatenate([bias_ref[...], jnp.zeros_like(bias_ref)], axis=0).astype(BF16)
    out_a[0, share + ev_share :, :edge_width] = bias
    sent_a = post("send", col_peers, a_sems, lambda target: out_a.at[target], in_a.at[col])
    loads[2].wait()
    acc_s[...] = node_ref[...].reshape(rows, width)
    total = out_a[col].astype(F32)
    for copy, (_, _, source) in zip(sent_a, col_peers):
        copy.wait_recv()
        total = total + in_a[source].astype(F32)
    small_s[row] = total[share:].astype(BF16)
    smalls = post("recv", row_peers, small_sems, lambda target: small_s.at[row], small_s.at[row])
    here = pl.ds(pl.multiple_of(col * share, share), share)
    mixed = nodes_ref[here, :].astype(F32) + dot(total[:share].astype(BF16), wo_ref[...])
    mix_s[col] = mixed.astype(BF16)
    mixes = post("send", col_peers, mix_sems, lambda target: mix_s.at[col], mix_s.at[col])
    for copy, (_, _, source) in zip(backs, row_peers):
        copy.wait_recv()
        asked = asked_ref[source][0:1, 0:1]
        landed = back_s[source].astype(F32)
        for at in range(blocks):
            acc_s[at * block : (at + 1) * block, :] += jnp.where(asked == float(at), landed, 0.0)
    for part in range(n_send):
        out_n[part] = acc_s[part * share : (part + 1) * share, :].astype(BF16)
    sent_n = post("send", col_peers, n_sems, lambda target: out_n.at[target], in_n.at[col])
    for copy in smalls:
        copy.wait_recv()
    small = small_s[0].astype(F32)
    for at in range(1, n_recv):
        small = small + small_s[at].astype(F32)
    small_all[col] = small.astype(BF16)
    small_alls = post(
        "send", col_peers, small_all_sems, lambda target: small_all.at[col], small_all.at[col]
    )
    total = out_n[col].astype(F32)
    for copy, (_, _, source) in zip(sent_n, col_peers):
        copy.wait_recv()
        total = total + in_n[source].astype(F32)
    fin_s[col] = total.astype(BF16)
    fins = post("send", col_peers, fin_sems, lambda target: fin_s.at[col], fin_s.at[col])
    for copy in mixes:
        copy.wait_recv()
    mixed_ref[...] = mix_s[...].reshape(rows, width)
    for copy in small_alls:
        copy.wait_recv()
    for part in range(n_send):
        ev_out_ref[part * ev_share : (part + 1) * ev_share, :] = small_all[part, :ev_share].astype(F32)
    bias_out_ref[...] = small_all[0, ev_share:, :edge_width].astype(F32)[:heads]
    for copy in fins:
        copy.wait_recv()
    for part in range(n_send):
        span = slice(part * share, (part + 1) * share)
        grad_ref[span, :] = dout_ref[span, :].astype(F32) + fin_s[part].astype(F32)
    for copy in backs + sent_a + smalls + mixes + sent_n + small_alls + fins:
        copy.wait_send()


def table_place(own_blocks, slot, pairs):
    owner = pairs[1, slot] // own_blocks
    return jnp.where(
        owner == pairs[0, slot] // own_blocks, pairs[1, slot] % own_blocks, own_blocks + owner
    )


def whole_spec(array):
    zeros = (0,) * array.ndim
    return pl.BlockSpec(array.shape, lambda slot, *_: zeros)


def slot_spec(shape):
    rest = (0,) * (len(shape) - 1)
    return pl.BlockSpec((1,) + tuple(shape[1:]), lambda slot, *_: (slot,) + rest)


def body(
    nodes,
    frames,
    pairs,
    masks,
    d_out,
    w_query,
    w_key,
    w_value,
    w_left,
    w_right,
    frame_edge,
    w_bias,
    w_edge_value,
    w_out,
):
    rows, width = nodes.shape
    slots, block = masks.shape
    nb_local = rows // block
    heads, edge_width = w_bias.shape
    att_width = w_query.shape[1]
    scale = (att_width // heads) ** (-0.5)
    n_recv = lax.axis_size("recv")
    n_send = lax.axis_size("send")

    node_blocks = nodes.reshape(nb_local, block, width)
    in_vmem = pl.BlockSpec(memory_space=pltpu.VMEM)
    in_hbm = pl.BlockSpec(memory_space=pltpu.HBM)
    asks_shape = (n_recv, 8, 128)
    table, asked = pl.pallas_call(
        functools.partial(fetch_kernel, n_recv),
        in_specs=[pl.BlockSpec(memory_space=pltpu.SMEM), in_vmem],
        out_specs=[in_vmem] * 2,
        out_shape=[
            jax.ShapeDtypeStruct((nb_local + n_recv, block, width), BF16),
            jax.ShapeDtypeStruct(asks_shape, F32),
        ],
        scratch_shapes=[
            pltpu.VMEM(asks_shape, F32),
            pltpu.VMEM(asks_shape, F32),
            pltpu.VMEM((n_recv, block, width), BF16),
            pltpu.VMEM((n_recv, block, width), BF16),
            pltpu.SemaphoreType.DMA((2, n_recv)),
            pltpu.SemaphoreType.DMA((2, n_recv)),
        ],
        compiler_params=pltpu.CompilerParams(
            collective_id=1, has_side_effects=True, vmem_limit_bytes=VMEM_LIMIT
        ),
        name="fetch",
    )(pairs, node_blocks)

    frame_rows = frames.reshape(-1, 1, block)
    mask_rows = masks.reshape(slots, 1, block)
    edge_row = frame_edge.reshape(1, edge_width)
    recv_spec = pl.BlockSpec((block, width), lambda slot, pairs, *_: (pairs[0, slot] % nb_local, 0))
    sender_spec = pl.BlockSpec(
        (1, block, width), lambda slot, pairs, *_: (table_place(nb_local, slot, pairs), 0, 0)
    )
    logit_shape = (slots, block, heads, block)
    sums_shape = (slots, block, 2 * heads, edge_width)
    slope_shape = (slots, block, block, edge_width)
    att_shape = (slots, block, att_width)
    stats_shape = (slots, 4, block * heads // 128, 128)
    weights = (w_query, w_key, w_value, w_left, w_right, edge_row, w_bias, w_edge_value, w_out)
    forward = pl.pallas_call(
        functools.partial(forward_kernel, scale, nb_local),
        grid_spec=pltpu.PrefetchScalarGridSpec(
            num_scalar_prefetch=2,
            grid=(slots,),
            in_specs=[
                pl.BlockSpec((1, 1, block), lambda slot, pairs, *_: (pairs[1, slot], 0, 0)),
                slot_spec(mask_rows.shape),
                recv_spec,
                recv_spec,
                sender_spec,
            ]
            + [whole_spec(weight) for weight in weights],
            out_specs=[
                slot_spec(shape)
                for shape in (
                    logit_shape, logit_shape, slope_shape, sums_shape, sums_shape, att_shape, stats_shape,
                )
            ],
            scratch_shapes=[
                pltpu.VMEM((block, edge_width), F32),
                pltpu.VMEM((block, block, edge_width), BF16),
                pltpu.VMEM((block * heads, block), BF16),
                pltpu.VMEM((block, heads, block), F32),
                pltpu.VMEM((block, heads, block), F32),
            ],
        ),
        out_shape=[
            jax.ShapeDtypeStruct(logit_shape, F32),
            jax.ShapeDtypeStruct(logit_shape, F32),
            jax.ShapeDtypeStruct(slope_shape, BF16),
            jax.ShapeDtypeStruct(sums_shape, BF16),
            jax.ShapeDtypeStruct(sums_shape, BF16),
            jax.ShapeDtypeStruct(att_shape, F32),
            jax.ShapeDtypeStruct(stats_shape, F32),
        ],
        compiler_params=pltpu.CompilerParams(vmem_limit_bytes=VMEM_LIMIT),
        name="forward",
    )
    logits, dprobs, slopes, sums, wides, att_parts, stats = forward(
        pairs, frames,
        frame_rows, mask_rows, nodes, d_out, table, *weights,
    )

    joined_shape = (slots, 2) + stats.shape[2:]
    joined = pl.pallas_call(
        functools.partial(join_kernel, n_send),
        in_specs=[in_vmem],
        out_specs=in_vmem,
        out_shape=jax.ShapeDtypeStruct(joined_shape, F32),
        scratch_shapes=[
            pltpu.VMEM((n_send,) + stats.shape, F32),
            pltpu.SemaphoreType.DMA((2, n_send)),
        ],
        compiler_params=pltpu.CompilerParams(
            collective_id=2, has_side_effects=True, vmem_limit_bytes=VMEM_LIMIT
        ),
        name="join",
    )(stats)

    weights = (w_query, w_key, w_value, w_left, w_right, w_out)
    node_shape = (nb_local, block, width)
    away_shape = (n_recv, block, width)
    att_sum_shape = (nb_local, block, att_width)
    backward = pl.pallas_call(
        functools.partial(backward_kernel, scale, nb_local),
        grid_spec=pltpu.PrefetchScalarGridSpec(
            num_scalar_prefetch=1,
            grid=(slots,),
            in_specs=[slot_spec(mask_rows.shape), recv_spec, recv_spec, sender_spec]
            + [whole_spec(weight) for weight in weights]
            + [
                slot_spec(shape)
                for shape in (
                    logit_shape, logit_shape, slope_shape, sums_shape, sums_shape, att_shape, stats_shape,
                    joined.shape,
                )
            ],
            out_specs=[
                whole_spec(node_blocks),
                whole_spec(jax.ShapeDtypeStruct(away_shape, BF16)),
                whole_spec(jax.ShapeDtypeStruct(att_sum_shape, F32)),
                whole_spec(w_edge_value),
                whole_spec(w_bias),
            ],
            scratch_shapes=[
                pltpu.VMEM((block * heads, block), BF16),
                pltpu.VMEM((block * heads, block), BF16),
                pltpu.VMEM((block * heads, edge_width), BF16),
                pltpu.VMEM((block, edge_width), F32),
                pltpu.VMEM((block, edge_width), F32),
                pltpu.VMEM((WIDE_CHUNK // GROUP, GROUP * 2 * heads, GROUP * edge_width), BF16),
            ],
        ),
        out_shape=[
            jax.ShapeDtypeStruct(node_shape, F32),
            jax.ShapeDtypeStruct(away_shape, BF16),
            jax.ShapeDtypeStruct(att_sum_shape, F32),
            jax.ShapeDtypeStruct(w_edge_value.shape, F32),
            jax.ShapeDtypeStruct(w_bias.shape, F32),
        ],
        compiler_params=pltpu.CompilerParams(vmem_limit_bytes=VMEM_LIMIT),
        name="backward",
    )
    node_sum, leaving, att, grad_ev, grad_bias = backward(
        pairs, mask_rows, nodes, d_out, table, *weights,
        logits, dprobs, slopes, sums, wides, att_parts, stats, joined,
    )

    share = rows // n_send
    ev_share = edge_width // n_send
    tail_rows = ev_share + BIAS_ROWS
    return pl.pallas_call(
        functools.partial(tail_kernel, n_recv, n_send),
        in_specs=[in_hbm, in_hbm, in_hbm, in_vmem, in_hbm, in_vmem, in_vmem, in_vmem, in_vmem],
        out_specs=[in_vmem] * 4,
        out_shape=[
            jax.ShapeDtypeStruct((rows, width), BF16),
            jax.ShapeDtypeStruct((rows, width), F32),
            jax.ShapeDtypeStruct((heads, edge_width), F32),
            jax.ShapeDtypeStruct((edge_width, att_width), F32),
        ],
        scratch_shapes=[
            pltpu.VMEM(att_sum_shape, F32),
            pltpu.VMEM(node_shape, F32),
            pltpu.VMEM((edge_width, att_width), F32),
            pltpu.SemaphoreType.DMA((3,)),
            pltpu.VMEM(away_shape, BF16),
            pltpu.VMEM((n_send, share + tail_rows, att_width), BF16),
            pltpu.VMEM((n_send, share + tail_rows, att_width), BF16),
            pltpu.VMEM((n_send, share, width), BF16),
            pltpu.VMEM((n_recv, tail_rows, att_width), BF16),
            pltpu.VMEM((n_send, tail_rows, att_width), BF16),
            pltpu.VMEM((rows, width), F32),
            pltpu.VMEM((n_send, share, width), BF16),
            pltpu.VMEM((n_send, share, width), BF16),
            pltpu.VMEM((n_send, share, width), BF16),
            pltpu.SemaphoreType.DMA((2, n_recv)),
            pltpu.SemaphoreType.DMA((2, n_send)),
            pltpu.SemaphoreType.DMA((2, n_send)),
            pltpu.SemaphoreType.DMA((2, n_recv)),
            pltpu.SemaphoreType.DMA((2, n_send)),
            pltpu.SemaphoreType.DMA((2, n_send)),
            pltpu.SemaphoreType.DMA((2, n_send)),
        ],
        compiler_params=pltpu.CompilerParams(
            collective_id=3, has_side_effects=True, vmem_limit_bytes=TAIL_LIMIT
        ),
        name="tail",
    )(att, node_sum, leaving, asked, grad_ev, grad_bias, nodes, d_out, w_out)


def solution(mesh):
    in_specs = (
        P("recv", None),
        P(),
        P(None, ("recv", "send")),
        P(("recv", "send"), None),
        P("recv", None),
        P(),
        P(),
        P(),
        P(),
        P(),
        P(),
        P(),
        P(),
        P(),
    )
    out_specs = (P("recv", None), P("recv", None), P(), P())
    return jax.shard_map(body, mesh=mesh, in_specs=in_specs, out_specs=out_specs, check_vma=False)
```

```python
import functools

import jax
import jax.numpy as jnp
from jax import lax
from jax.experimental import pallas as pl
from jax.experimental.pallas import tpu as pltpu
from jax.sharding import PartitionSpec as P

NEG_LARGE = -1e30
CHUNK = 16
WIDE_CHUNK = 32
GROUP = 8
BIAS_ROWS = 16
VMEM_LIMIT = 60 * 2**20
TAIL_LIMIT = 40 * 2**20
BACKWARD_LIMIT = 50 * 2**20
F32 = jnp.float32
BF16 = jnp.bfloat16


def dot(first, second, first_dim=1, second_dim=0):
    return lax.dot_general(
        first, second, (((first_dim,), (second_dim,)), ((), ())), preferred_element_type=F32
    )


def to_column(row):
    count = row.shape[1]
    eye = lax.broadcasted_iota(jnp.int32, (count, count), 0) == lax.broadcasted_iota(
        jnp.int32, (count, count), 1
    )
    return jnp.sum(jnp.where(eye, row, 0.0), axis=1, keepdims=True)


def to_row(column):
    count = column.shape[0]
    eye = lax.broadcasted_iota(jnp.int32, (count, count), 0) == lax.broadcasted_iota(
        jnp.int32, (count, count), 1
    )
    return jnp.sum(jnp.where(eye, column, 0.0), axis=0, keepdims=True)


def head_mask(heads, width):
    return lax.broadcasted_iota(jnp.int32, (heads, width), 1) // (
        width // heads
    ) == lax.broadcasted_iota(jnp.int32, (heads, width), 0)


def owner_matrix(count, heads, rows_first):
    shape = (count * heads, count) if rows_first else (count, count * heads)
    wide = lax.broadcasted_iota(jnp.int32, shape, 0 if rows_first else 1) // heads
    narrow = lax.broadcasted_iota(jnp.int32, shape, 1 if rows_first else 0)
    return jnp.where(wide == narrow, 1.0, 0.0).astype(BF16)


def spread(rows, heads):
    count, width = rows.shape
    mask = head_mask(heads, width)
    wide = dot(owner_matrix(count, heads, True), rows).reshape(count, heads, width)
    return jnp.where(mask[None], wide, 0.0).reshape(count * heads, width).astype(BF16)


def gather_heads(wide, heads):
    count, width = wide.shape
    mask = head_mask(heads, width)
    kept = jnp.where(mask[None], wide.reshape(count // heads, heads, width), 0.0)
    return dot(owner_matrix(count // heads, heads, False), kept.reshape(count, width).astype(BF16))


def forward_kernel(
    scale,
    own_blocks,
    pairs_ref,
    frames_ref,
    frame_row_ref,
    mask_ref,
    nodes_ref,
    dout_ref,
    sender_ref,
    wq_ref,
    wk_ref,
    wv_ref,
    wl_ref,
    wr_ref,
    fe_ref,
    wb_ref,
    wev_ref,
    wo_ref,
    logit_ref,
    dprob_ref,
    slope_ref,
    sums_ref,
    wide_ref,
    att_ref,
    stats_ref,
    left_s,
    edge_s,
    probs_s,
    scores_s,
    dvalues_s,
):
    slot = pl.program_id(0)
    heads, edge_width = wb_ref.shape
    block = nodes_ref.shape[0]
    nodes = nodes_ref[...]
    sender = sender_ref[0]
    query = dot(nodes, wq_ref[...]).astype(BF16)
    left_s[...] = dot(nodes, wl_ref[...]) * 0.5
    datt = dot(dout_ref[...], wo_ref[...], 1, 1).astype(BF16)
    keys = dot(sender, wk_ref[...]).astype(BF16)
    values = dot(sender, wv_ref[...]).astype(BF16)
    right = dot(sender, wr_ref[...]) * 0.5
    right_same = (right + fe_ref[...].astype(F32) * 0.5).astype(BF16)
    right = right.astype(BF16)
    frame_col = jnp.broadcast_to(
        to_column(frame_row_ref[0].astype(F32)), (block, edge_width)
    ).astype(BF16)
    datt_wide = spread(datt, heads)
    scores_s[...] = (dot(spread(query, heads), keys, 1, 1) * scale).reshape(block, heads, block)
    dvalues_s[...] = dot(datt_wide, values, 1, 1).reshape(block, heads, block)
    dctx = dot(datt_wide, wev_ref[...], 1, 1).reshape(block, heads, edge_width)
    bias = jnp.broadcast_to(wb_ref[...].astype(F32)[None], dctx.shape)
    wide_ref[0] = jnp.concatenate([bias, dctx], axis=1).astype(BF16)
    recv_start = pairs_ref[0, slot] * block

    one = jnp.ones((), BF16)

    def edge_step(group, carry):
        start = group * WIDE_CHUNK
        left_rows = left_s[pl.ds(start, WIDE_CHUNK), :].astype(BF16)
        for step in range(0, WIDE_CHUNK, 2):
            edges = []
            for at in (step, step + 1):
                frame = frames_ref[recv_start + start + at].astype(F32).astype(BF16)
                half = left_rows[at : at + 1] + jnp.where(frame_col == frame, right_same, right)
                turn = jnp.tanh(half)
                gain = half * turn
                edge = half + gain
                slope_ref[0, start + at] = (one + turn) * (one + (half - gain))
                edge_s[start + at] = edge
                edges.append(edge)
            wide = wide_ref[0, pl.ds(start + step, 2)].reshape(4 * heads, edge_width)
            both = dot(wide, jnp.concatenate(edges, axis=0), 1, 1)
            for at in (0, 1):
                part = both[2 * heads * at : 2 * heads * (at + 1), block * at : block * (at + 1)]
                here = start + step + at
                logit_ref[0, here] = scores_s[here] + part[:heads]
                dprob_ref[0, here] = dvalues_s[here] + part[heads:]
        return carry

    lax.fori_loop(0, block // WIDE_CHUNK, edge_step, 0)
    valid = mask_ref[0] > 0

    def soft_step(step_at, carry):
        for sub in range(WIDE_CHUNK // CHUNK):
            group = step_at * (WIDE_CHUNK // CHUNK) + sub
            start = group * CHUNK
            rows = pl.ds(start * heads, CHUNK * heads)
            logits = logit_ref[0, pl.ds(start, CHUNK)].reshape(CHUNK * heads, block)
            dprob = dprob_ref[0, pl.ds(start, CHUNK)].reshape(CHUNK * heads, block)
            logits = jnp.where(valid, logits, NEG_LARGE)
            top = jnp.max(logits, axis=1, keepdims=True)
            probs = jnp.where(valid, jnp.exp(logits - top), 0.0)
            weighted = probs * dprob
            stats_ref[0, 0, pl.ds(group, 1), :] = to_row(top)
            stats_ref[0, 1, pl.ds(group, 1), :] = to_row(jnp.sum(probs, axis=1, keepdims=True))
            stats_ref[0, 2, pl.ds(group, 1), :] = to_row(jnp.sum(weighted, axis=1, keepdims=True))
            probs_s[rows, :] = probs.astype(BF16)
            pair = jnp.concatenate(
                [probs.reshape(CHUNK, heads, block), weighted.reshape(CHUNK, heads, block)], axis=1
            ).astype(BF16)
            for step in range(0, CHUNK, 2):
                edges = jnp.concatenate([edge_s[start + step], edge_s[start + step + 1]], axis=1)
                both = dot(pair[step : step + 2].reshape(4 * heads, block), edges).astype(BF16)
                sums_ref[0, start + step] = both[: 2 * heads, :edge_width]
                sums_ref[0, start + step + 1] = both[2 * heads :, edge_width:]
        return carry

    lax.fori_loop(0, block // WIDE_CHUNK, soft_step, 0)
    stats_ref[0, 3] = jnp.full(stats_ref.shape[2:], pairs_ref[0, slot].astype(F32), F32)
    ctx = sums_ref[0].astype(F32)[:, :heads].reshape(block * heads, edge_width).astype(BF16)
    att_ref[0] = gather_heads(dot(probs_s[...], values) + dot(ctx, wev_ref[...]), heads)


def backward_kernel(
    scale,
    own_blocks,
    pairs_ref,
    mask_ref,
    nodes_ref,
    dout_ref,
    sender_ref,
    wq_ref,
    wk_ref,
    wv_ref,
    wl_ref,
    wr_ref,
    wo_ref,
    logit_ref,
    dprob_ref,
    slope_ref,
    sums_ref,
    wide_ref,
    att_in_ref,
    stats_ref,
    joined_ref,
    node_ref,
    leaving_ref,
    att_ref,
    grad_ev_ref,
    grad_bias_ref,
    probs_s,
    dlogit_s,
    ctx_s,
    left_s,
    right_s,
    diagonal_s,
):
    slot = pl.program_id(0)
    heads = logit_ref.shape[2]
    block = nodes_ref.shape[0]
    edge_width = wide_ref.shape[3]
    width = wq_ref.shape[1]
    mask = head_mask(heads, width)
    valid = mask_ref[0] > 0

    @pl.when(slot == 0)
    def _():
        grad_ev_ref[...] = jnp.zeros_like(grad_ev_ref)
        grad_bias_ref[...] = jnp.zeros_like(grad_bias_ref)
        node_ref[...] = jnp.zeros_like(node_ref)
        diagonal_s[...] = jnp.zeros_like(diagonal_s)
        leaving_ref[...] = jnp.zeros_like(leaving_ref)
        att_ref[...] = jnp.zeros_like(att_ref)

    local = pairs_ref[0, slot] % own_blocks
    place = table_place(own_blocks, slot, pairs_ref)
    right_s[...] = jnp.zeros_like(right_s)

    def step_group(step_at, carry):
        for sub in range(WIDE_CHUNK // CHUNK):
            group = step_at * (WIDE_CHUNK // CHUNK) + sub
            start = group * CHUNK
            rows = pl.ds(start * heads, CHUNK * heads)
            lse = joined_ref[0, 0, pl.ds(group, 1), :]
            lse_col = to_column(lse)
            delta_col = to_column(joined_ref[0, 1, pl.ds(group, 1), :])
            factor_col = to_column(jnp.exp(stats_ref[0, 0, pl.ds(group, 1), :] - lse))
            logits = logit_ref[0, pl.ds(start, CHUNK)].reshape(CHUNK * heads, block)
            dprob = dprob_ref[0, pl.ds(start, CHUNK)].reshape(CHUNK * heads, block)
            probs = jnp.where(valid, jnp.exp(logits - lse_col), 0.0)
            dlogit = probs * (dprob - delta_col)
            probs_s[rows, :] = probs.astype(BF16)
            dlogit_s[rows, :] = dlogit.astype(BF16)
            sums = sums_ref[0, pl.ds(start, CHUNK)].astype(F32)
            ctx = sums[:, :heads].reshape(CHUNK * heads, edge_width) * factor_col
            ctx_s[rows, :] = ctx.astype(BF16)
            moved = sums[:, heads:].reshape(CHUNK * heads, edge_width) * factor_col - ctx * delta_col
            grad_bias_ref[...] += jnp.sum(moved.reshape(CHUNK, heads, edge_width), axis=0)
            factor = jnp.sum(
                jnp.where(mask[None], factor_col.reshape(CHUNK, heads, 1), 0.0), axis=1
            )
            att_ref[local, pl.ds(start, CHUNK), :] += att_in_ref[0, pl.ds(start, CHUNK), :] * factor
            pair = jnp.concatenate(
                [dlogit.reshape(CHUNK, heads, block), probs.reshape(CHUNK, heads, block)], axis=1
            ).astype(BF16)
            right_sum = right_s[...]
            lefts = []
            for half in range(CHUNK // GROUP):
                first = half * GROUP
                for step in range(GROUP):
                    diagonal_s[
                        sub * (CHUNK // GROUP) + half,
                        2 * heads * step : 2 * heads * (step + 1),
                        edge_width * step : edge_width * (step + 1),
                    ] = wide_ref[0, start + first + step]
                pairs = pair[first : first + GROUP].reshape(GROUP * 2 * heads, block)
                d_edges = dot(pairs, diagonal_s[sub * (CHUNK // GROUP) + half], 0, 0)
                for step in range(GROUP):
                    slope = slope_ref[0, start + first + step].astype(F32)
                    d_pre = d_edges[:, edge_width * step : edge_width * (step + 1)] * slope
                    right_sum = right_sum + d_pre
                    lefts.append(jnp.sum(d_pre, axis=0, keepdims=True))
            right_s[...] = right_sum
            left_s[pl.ds(start, CHUNK), :] = jnp.concatenate(lefts, axis=0)
        return carry

    lax.fori_loop(0, block // WIDE_CHUNK, step_group, 0)
    nodes = nodes_ref[...]
    sender = sender_ref[0]
    query_wide = spread(dot(nodes, wq_ref[...]).astype(BF16), heads)
    datt_wide = spread(dot(dout_ref[...], wo_ref[...], 1, 1).astype(BF16), heads)
    keys = dot(sender, wk_ref[...]).astype(BF16)
    dlogit = dlogit_s[...]
    grad_query = gather_heads(dot(dlogit, keys), heads) * scale
    grad_keys = dot(dlogit, query_wide, 0, 0) * scale
    grad_values = dot(probs_s[...], datt_wide, 0, 0)
    node_ref[local] += dot(grad_query.astype(BF16), wq_ref[...], 1, 1) + 0.5 * dot(
        left_s[...].astype(BF16), wl_ref[...], 1, 1
    )
    send_grad = (
        dot(grad_keys.astype(BF16), wk_ref[...], 1, 1)
        + dot(grad_values.astype(BF16), wv_ref[...], 1, 1)
        + 0.5 * dot(right_s[...].astype(BF16), wr_ref[...], 1, 1)
    )

    @pl.when(place < own_blocks)
    def _():
        node_ref[place] += send_grad

    @pl.when(place >= own_blocks)
    def _():
        leaving_ref[place - own_blocks] = send_grad.astype(BF16)

    grad_ev_ref[...] += dot(ctx_s[...], datt_wide, 0, 0)


MESH = pl.DeviceIdType.MESH


def peers_of(axis, count):
    me = lax.axis_index(axis)
    return me, [
        (offset, lax.rem(me + offset, count), lax.rem(me + count - offset, count))
        for offset in range(1, count)
    ]


def meet(groups):
    barrier = pltpu.get_barrier_semaphore()
    total = 0
    for axis, peers in groups:
        for _, target, _ in peers:
            pl.semaphore_signal(barrier, inc=1, device_id={axis: target}, device_id_type=MESH)
            total += 1
    pl.semaphore_wait(barrier, total)


def post(axis, peers, sems, source, landing):
    copies = []
    for offset, target, _ in peers:
        copy = pltpu.make_async_remote_copy(
            src_ref=source(target),
            dst_ref=landing,
            send_sem=sems.at[0, offset],
            recv_sem=sems.at[1, offset],
            device_id={axis: target},
            device_id_type=MESH,
        )
        copy.start()
        copies.append(copy)
    return copies


def fetch_kernel(
    n_recv, pairs_ref, nodes_ref, table_ref, asked_ref, want_s, ask_s, reply_s, got_s, ask_sems, reply_sems
):
    me, peers = peers_of("recv", n_recv)
    blocks = nodes_ref.shape[0]
    for _, target, _ in peers:
        wanted = 0
        for slot in range(pairs_ref.shape[1]):
            sender = pairs_ref[1, slot]
            wanted = wanted + jnp.where(sender // blocks == target, sender % blocks, 0)
        want_s[target] = jnp.full(want_s.shape[1:], wanted, jnp.int32).astype(F32)
    meet([("recv", peers)])
    asks = post("recv", peers, ask_sems, lambda target: want_s.at[target], ask_s.at[me])
    nodes = nodes_ref[...].astype(F32)
    for copy in asks:
        copy.wait_recv()
    replies = []
    for peer in peers:
        offset, target, _ = peer
        ask = ask_s[target][0:1, 0:1]
        reply = nodes[0]
        for at in range(1, nodes.shape[0]):
            reply = jnp.where(ask == float(at), nodes[at], reply)
        reply_s[offset] = reply.astype(BF16)
        replies += post("recv", [peer], reply_sems, lambda target: reply_s.at[offset], got_s.at[me])
    asked_ref[...] = jnp.zeros_like(asked_ref)
    table_ref[:blocks] = nodes_ref[...]
    table_ref[blocks + me] = jnp.zeros_like(nodes_ref[0])
    for _, target, _ in peers:
        asked_ref[target] = ask_s[target]
    for copy, (_, _, source) in zip(replies, peers):
        copy.wait_recv()
        table_ref[blocks + source] = got_s[source]
    for copy in asks + replies:
        copy.wait_send()


def join_kernel(n_send, stats_ref, joined_ref, all_s, sems):
    me, peers = peers_of("send", n_send)
    meet([("send", peers)])
    copies = post("send", peers, sems, lambda target: stats_ref, all_s.at[me])
    slots = stats_ref.shape[0]
    all_s[me] = stats_ref[...]
    for copy in copies:
        copy.wait_recv()
    for slot in range(slots):
        lands = stats_ref[slot, 3]
        top = stats_ref[slot, 0]
        for device in range(n_send):
            for other in range(slots):
                top = jnp.maximum(
                    top,
                    jnp.where(all_s[device, other, 3] == lands, all_s[device, other, 0], NEG_LARGE),
                )
        total = jnp.zeros_like(top)
        delta = jnp.zeros_like(top)
        for device in range(n_send):
            for other in range(slots):
                part = jnp.where(
                    all_s[device, other, 3] == lands, jnp.exp(all_s[device, other, 0] - top), 0.0
                )
                total = total + part * all_s[device, other, 1]
                delta = delta + part * all_s[device, other, 2]
        joined_ref[slot, 0] = top + jnp.log(total)
        joined_ref[slot, 1] = delta / total
    for copy in copies:
        copy.wait_send()


def tail_kernel(
    n_recv,
    n_send,
    att_hbm,
    node_hbm,
    leaving_ref,
    asked_ref,
    ev_hbm,
    bias_ref,
    nodes_ref,
    dout_ref,
    wo_ref,
    mixed_ref,
    grad_ref,
    bias_out_ref,
    ev_out_ref,
    att_ref,
    node_ref,
    ev_ref,
    load_sems,
    back_s,
    out_a,
    in_a,
    mix_s,
    small_s,
    small_all,
    acc_s,
    out_n,
    in_n,
    fin_s,
    back_sems,
    a_sems,
    mix_sems,
    small_sems,
    small_all_sems,
    n_sems,
    fin_sems,
):
    row, row_peers = peers_of("recv", n_recv)
    col, col_peers = peers_of("send", n_send)
    blocks, block, width = node_ref.shape
    rows = blocks * block
    share = rows // n_send
    ev_share = ev_ref.shape[0] // n_send
    heads, edge_width = bias_ref.shape
    loads = [
        pltpu.make_async_copy(source, target, load_sems.at[at])
        for at, (source, target) in enumerate(
            ((att_hbm, att_ref), (ev_hbm, ev_ref), (node_hbm, node_ref))
        )
    ]
    for load in loads:
        load.start()
    meet([("recv", row_peers), ("send", col_peers)])
    backs = post("recv", row_peers, back_sems, lambda target: leaving_ref.at[target], back_s.at[row])
    loads[0].wait()
    loads[1].wait()
    sums = att_ref[...].reshape(rows, width)
    for part in range(n_send):
        out_a[part, :share] = sums[part * share : (part + 1) * share].astype(BF16)
        out_a[part, share : share + ev_share] = ev_ref[
            part * ev_share : (part + 1) * ev_share
        ].astype(BF16)
        out_a[part, share + ev_share :] = jnp.zeros((BIAS_ROWS, width), BF16)
    bias = jnp.concatenate([bias_ref[...], jnp.zeros_like(bias_ref)], axis=0).astype(BF16)
    out_a[0, share + ev_share :, :edge_width] = bias
    sent_a = post("send", col_peers, a_sems, lambda target: out_a.at[target], in_a.at[col])
    loads[2].wait()
    acc_s[...] = node_ref[...].reshape(rows, width)
    total = out_a[col].astype(F32)
    for copy, (_, _, source) in zip(sent_a, col_peers):
        copy.wait_recv()
        total = total + in_a[source].astype(F32)
    small_s[row] = total[share:].astype(BF16)
    smalls = post("recv", row_peers, small_sems, lambda target: small_s.at[row], small_s.at[row])
    here = pl.ds(pl.multiple_of(col * share, share), share)
    mixed = nodes_ref[here, :].astype(F32) + dot(total[:share].astype(BF16), wo_ref[...])
    mix_s[col] = mixed.astype(BF16)
    mixes = post("send", col_peers, mix_sems, lambda target: mix_s.at[col], mix_s.at[col])
    for copy, (_, _, source) in zip(backs, row_peers):
        copy.wait_recv()
        asked = asked_ref[source][0:1, 0:1]
        landed = back_s[source].astype(F32)
        for at in range(blocks):
            acc_s[at * block : (at + 1) * block, :] += jnp.where(asked == float(at), landed, 0.0)
    for part in range(n_send):
        out_n[part] = acc_s[part * share : (part + 1) * share, :].astype(BF16)
    sent_n = post("send", col_peers, n_sems, lambda target: out_n.at[target], in_n.at[col])
    for copy in smalls:
        copy.wait_recv()
    small = small_s[0].astype(F32)
    for at in range(1, n_recv):
        small = small + small_s[at].astype(F32)
    small_all[col] = small.astype(BF16)
    small_alls = post(
        "send", col_peers, small_all_sems, lambda target: small_all.at[col], small_all.at[col]
    )
    total = out_n[col].astype(F32)
    for copy, (_, _, source) in zip(sent_n, col_peers):
        copy.wait_recv()
        total = total + in_n[source].astype(F32)
    fin_s[col] = total.astype(BF16)
    fins = post("send", col_peers, fin_sems, lambda target: fin_s.at[col], fin_s.at[col])
    for copy in mixes:
        copy.wait_recv()
    mixed_ref[...] = mix_s[...].reshape(rows, width)
    for copy in small_alls:
        copy.wait_recv()
    for part in range(n_send):
        ev_out_ref[part * ev_share : (part + 1) * ev_share, :] = small_all[part, :ev_share].astype(F32)
    bias_out_ref[...] = small_all[0, ev_share:, :edge_width].astype(F32)[:heads]
    for copy in fins:
        copy.wait_recv()
    for part in range(n_send):
        span = slice(part * share, (part + 1) * share)
        grad_ref[span, :] = dout_ref[span, :].astype(F32) + fin_s[part].astype(F32)
    for copy in backs + sent_a + smalls + mixes + sent_n + small_alls + fins:
        copy.wait_send()


def table_place(own_blocks, slot, pairs):
    owner = pairs[1, slot] // own_blocks
    return jnp.where(
        owner == pairs[0, slot] // own_blocks, pairs[1, slot] % own_blocks, own_blocks + owner
    )


def whole_spec(array):
    zeros = (0,) * array.ndim
    return pl.BlockSpec(array.shape, lambda slot, *_: zeros)


def slot_spec(shape):
    rest = (0,) * (len(shape) - 1)
    return pl.BlockSpec((1,) + tuple(shape[1:]), lambda slot, *_: (slot,) + rest)


def body(
    nodes,
    frames,
    pairs,
    masks,
    d_out,
    w_query,
    w_key,
    w_value,
    w_left,
    w_right,
    frame_edge,
    w_bias,
    w_edge_value,
    w_out,
):
    rows, width = nodes.shape
    slots, block = masks.shape
    nb_local = rows // block
    heads, edge_width = w_bias.shape
    att_width = w_query.shape[1]
    scale = (att_width // heads) ** (-0.5)
    n_recv = lax.axis_size("recv")
    n_send = lax.axis_size("send")

    node_blocks = nodes.reshape(nb_local, block, width)
    in_vmem = pl.BlockSpec(memory_space=pltpu.VMEM)
    in_hbm = pl.BlockSpec(memory_space=pltpu.HBM)
    asks_shape = (n_recv, 8, 128)
    table, asked = pl.pallas_call(
        functools.partial(fetch_kernel, n_recv),
        in_specs=[pl.BlockSpec(memory_space=pltpu.SMEM), in_vmem],
        out_specs=[in_vmem] * 2,
        out_shape=[
            jax.ShapeDtypeStruct((nb_local + n_recv, block, width), BF16),
            jax.ShapeDtypeStruct(asks_shape, F32),
        ],
        scratch_shapes=[
            pltpu.VMEM(asks_shape, F32),
            pltpu.VMEM(asks_shape, F32),
            pltpu.VMEM((n_recv, block, width), BF16),
            pltpu.VMEM((n_recv, block, width), BF16),
            pltpu.SemaphoreType.DMA((2, n_recv)),
            pltpu.SemaphoreType.DMA((2, n_recv)),
        ],
        compiler_params=pltpu.CompilerParams(
            collective_id=1, has_side_effects=True, vmem_limit_bytes=VMEM_LIMIT
        ),
        name="fetch",
    )(pairs, node_blocks)

    frame_rows = frames.reshape(-1, 1, block)
    mask_rows = masks.reshape(slots, 1, block)
    edge_row = frame_edge.reshape(1, edge_width)
    recv_spec = pl.BlockSpec((block, width), lambda slot, pairs, *_: (pairs[0, slot] % nb_local, 0))
    sender_spec = pl.BlockSpec(
        (1, block, width), lambda slot, pairs, *_: (table_place(nb_local, slot, pairs), 0, 0)
    )
    logit_shape = (slots, block, heads, block)
    sums_shape = (slots, block, 2 * heads, edge_width)
    slope_shape = (slots, block, block, edge_width)
    att_shape = (slots, block, att_width)
    stats_shape = (slots, 4, block * heads // 128, 128)
    weights = (w_query, w_key, w_value, w_left, w_right, edge_row, w_bias, w_edge_value, w_out)
    forward = pl.pallas_call(
        functools.partial(forward_kernel, scale, nb_local),
        grid_spec=pltpu.PrefetchScalarGridSpec(
            num_scalar_prefetch=2,
            grid=(slots,),
            in_specs=[
                pl.BlockSpec((1, 1, block), lambda slot, pairs, *_: (pairs[1, slot], 0, 0)),
                slot_spec(mask_rows.shape),
                recv_spec,
                recv_spec,
                sender_spec,
            ]
            + [whole_spec(weight) for weight in weights],
            out_specs=[
                slot_spec(shape)
                for shape in (
                    logit_shape, logit_shape, slope_shape, sums_shape, sums_shape, att_shape, stats_shape,
                )
            ],
            scratch_shapes=[
                pltpu.VMEM((block, edge_width), F32),
                pltpu.VMEM((block, block, edge_width), BF16),
                pltpu.VMEM((block * heads, block), BF16),
                pltpu.VMEM((block, heads, block), F32),
                pltpu.VMEM((block, heads, block), F32),
            ],
        ),
        out_shape=[
            jax.ShapeDtypeStruct(logit_shape, F32),
            jax.ShapeDtypeStruct(logit_shape, F32),
            jax.ShapeDtypeStruct(slope_shape, BF16),
            jax.ShapeDtypeStruct(sums_shape, BF16),
            jax.ShapeDtypeStruct(sums_shape, BF16),
            jax.ShapeDtypeStruct(att_shape, F32),
            jax.ShapeDtypeStruct(stats_shape, F32),
        ],
        compiler_params=pltpu.CompilerParams(vmem_limit_bytes=VMEM_LIMIT),
        name="forward",
    )
    logits, dprobs, slopes, sums, wides, att_parts, stats = forward(
        pairs, frames,
        frame_rows, mask_rows, nodes, d_out, table, *weights,
    )

    joined_shape = (slots, 2) + stats.shape[2:]
    joined = pl.pallas_call(
        functools.partial(join_kernel, n_send),
        in_specs=[in_vmem],
        out_specs=in_vmem,
        out_shape=jax.ShapeDtypeStruct(joined_shape, F32),
        scratch_shapes=[
            pltpu.VMEM((n_send,) + stats.shape, F32),
            pltpu.SemaphoreType.DMA((2, n_send)),
        ],
        compiler_params=pltpu.CompilerParams(
            collective_id=2, has_side_effects=True, vmem_limit_bytes=VMEM_LIMIT
        ),
        name="join",
    )(stats)

    weights = (w_query, w_key, w_value, w_left, w_right, w_out)
    node_shape = (nb_local, block, width)
    away_shape = (n_recv, block, width)
    att_sum_shape = (nb_local, block, att_width)
    backward = pl.pallas_call(
        functools.partial(backward_kernel, scale, nb_local),
        grid_spec=pltpu.PrefetchScalarGridSpec(
            num_scalar_prefetch=1,
            grid=(slots,),
            in_specs=[slot_spec(mask_rows.shape), recv_spec, recv_spec, sender_spec]
            + [whole_spec(weight) for weight in weights]
            + [
                slot_spec(shape)
                for shape in (
                    logit_shape, logit_shape, slope_shape, sums_shape, sums_shape, att_shape, stats_shape,
                    joined.shape,
                )
            ],
            out_specs=[
                whole_spec(node_blocks),
                whole_spec(jax.ShapeDtypeStruct(away_shape, BF16)),
                whole_spec(jax.ShapeDtypeStruct(att_sum_shape, F32)),
                whole_spec(w_edge_value),
                whole_spec(w_bias),
            ],
            scratch_shapes=[
                pltpu.VMEM((block * heads, block), BF16),
                pltpu.VMEM((block * heads, block), BF16),
                pltpu.VMEM((block * heads, edge_width), BF16),
                pltpu.VMEM((block, edge_width), F32),
                pltpu.VMEM((block, edge_width), F32),
                pltpu.VMEM((WIDE_CHUNK // GROUP, GROUP * 2 * heads, GROUP * edge_width), BF16),
            ],
        ),
        out_shape=[
            jax.ShapeDtypeStruct(node_shape, F32),
            jax.ShapeDtypeStruct(away_shape, BF16),
            jax.ShapeDtypeStruct(att_sum_shape, F32),
            jax.ShapeDtypeStruct(w_edge_value.shape, F32),
            jax.ShapeDtypeStruct(w_bias.shape, F32),
        ],
        compiler_params=pltpu.CompilerParams(vmem_limit_bytes=BACKWARD_LIMIT),
        name="backward",
    )
    node_sum, leaving, att, grad_ev, grad_bias = backward(
        pairs, mask_rows, nodes, d_out, table, *weights,
        logits, dprobs, slopes, sums, wides, att_parts, stats, joined,
    )

    share = rows // n_send
    ev_share = edge_width // n_send
    tail_rows = ev_share + BIAS_ROWS
    return pl.pallas_call(
        functools.partial(tail_kernel, n_recv, n_send),
        in_specs=[in_hbm, in_hbm, in_hbm, in_vmem, in_hbm, in_vmem, in_vmem, in_vmem, in_vmem],
        out_specs=[in_vmem] * 4,
        out_shape=[
            jax.ShapeDtypeStruct((rows, width), BF16),
            jax.ShapeDtypeStruct((rows, width), F32),
            jax.ShapeDtypeStruct((heads, edge_width), F32),
            jax.ShapeDtypeStruct((edge_width, att_width), F32),
        ],
        scratch_shapes=[
            pltpu.VMEM(att_sum_shape, F32),
            pltpu.VMEM(node_shape, F32),
            pltpu.VMEM((edge_width, att_width), F32),
            pltpu.SemaphoreType.DMA((3,)),
            pltpu.VMEM(away_shape, BF16),
            pltpu.VMEM((n_send, share + tail_rows, att_width), BF16),
            pltpu.VMEM((n_send, share + tail_rows, att_width), BF16),
            pltpu.VMEM((n_send, share, width), BF16),
            pltpu.VMEM((n_recv, tail_rows, att_width), BF16),
            pltpu.VMEM((n_send, tail_rows, att_width), BF16),
            pltpu.VMEM((rows, width), F32),
            pltpu.VMEM((n_send, share, width), BF16),
            pltpu.VMEM((n_send, share, width), BF16),
            pltpu.VMEM((n_send, share, width), BF16),
            pltpu.SemaphoreType.DMA((2, n_recv)),
            pltpu.SemaphoreType.DMA((2, n_send)),
            pltpu.SemaphoreType.DMA((2, n_send)),
            pltpu.SemaphoreType.DMA((2, n_recv)),
            pltpu.SemaphoreType.DMA((2, n_send)),
            pltpu.SemaphoreType.DMA((2, n_send)),
            pltpu.SemaphoreType.DMA((2, n_send)),
        ],
        compiler_params=pltpu.CompilerParams(
            collective_id=3, has_side_effects=True, vmem_limit_bytes=TAIL_LIMIT
        ),
        name="tail",
    )(att, node_sum, leaving, asked, grad_ev, grad_bias, nodes, d_out, w_out)


def solution(mesh):
    in_specs = (
        P("recv", None),
        P(),
        P(None, ("recv", "send")),
        P(("recv", "send"), None),
        P("recv", None),
        P(),
        P(),
        P(),
        P(),
        P(),
        P(),
        P(),
        P(),
        P(),
    )
    out_specs = (P("recv", None), P("recv", None), P(), P())
    return jax.shard_map(body, mesh=mesh, in_specs=in_specs, out_specs=out_specs, check_vma=False)
```
